128 devices in a mesh: space: 64 (over z, y, x), view: 2 (over core).
Axes of the slice: x: 4, y: 4, z: 4, core: 2. Of those that a mesh axis runs over, the one named last changes fastest.
Arguments:
- params: float32 [59, 131072], P(None, 'space')
- camera: float32 [2, 3, 4], P('view'), as said below
- eye_point: float32 [2, 3], P('view'), may hold values from -9 to 9
- tile_of: int32 [2, 512], P('view', 'space'), may hold values from 0 to 511, as said below
- fetch: int32 [2, 64, 64, 16], P('view', 'space'), may hold values from 0 to 2047, as said below
- lists: int32 [2, 512, 256], P('view', 'space'), may hold values from 0 to 1023
- counts: int32 [2, 512], P('view', 'space'), may hold values from 1 to 256
- target: float32 [2, 512, 3, 256], P('view', 'space'), may hold values from -2 to 2
Outputs:
- rendered: float32 [2, 512, 3, 256], P('view', 'space')
- grads: float32 [59, 131072], P(None, 'space')
The draws below stay inside these ranges and needn't reach their ends.
Inputs may be any that keep to these rules, and one draw needn't show every extreme that they name: `fetch`: over both views and all renderers, the entries for one owner name each of its 2048 Gaussians exactly once. `tile_of`: each view's row names every tile once; the slots of one renderer cover a rectangle of adjacent tiles. `camera`: in rows 0 and 1, columns 0 and 1 hold diagonal entries of 0.6 to 1.1 and off-diagonal entries of magnitude at most 0.4.
All inputs are finite; a program needn't handle non-finite values.
Results may differ from the reference program's by a relative error of at most 0.0003.
Values sent between devices are 32-bit elements; how exact they have to be, the bound alone decides.
A program may use at most 192 MiB of HBM per device.

```python
import jax
import jax.numpy as jnp
from jax import lax

G_DEV = 2048
TILES_DEV = 8
K = 256
CAP = 16
G = 131072
SLOTS = 512
VIEWS = 2
N_SPACE = 64


def tiling():
    log_tiles = TILES_DEV.bit_length() - 1
    block_wide = 1 << (log_tiles + 1) // 2
    return (block_wide, TILES_DEV // block_wide)


def owner_orders(key):
    base = jax.random.fold_in(key, 101)
    streams = jax.random.split(base, N_SPACE)
    orders = jax.vmap(lambda stream: jax.random.permutation(stream, G_DEV))(streams)
    return orders.astype(jnp.int32)


def block_orders(key):
    base = jax.random.fold_in(key, 103)
    streams = jax.random.split(base, VIEWS)
    orders = jax.vmap(lambda stream: jax.random.permutation(stream, N_SPACE))(streams)
    return orders.astype(jnp.int32)


def camera_rows(key):
    base = jax.random.fold_in(key, 107)
    streams = jax.random.split(base, 4)
    diagonal = jax.random.uniform(streams[0], (VIEWS, 2), jnp.float32, 0.6, 1.1)
    crossed = jax.random.uniform(streams[1], (VIEWS, 2), jnp.float32, -0.4, 0.4)
    depth_terms = jax.random.uniform(streams[2], (VIEWS, 2), jnp.float32, -0.4, 0.4)
    shifts = jax.random.uniform(streams[3], (VIEWS, 2), jnp.float32, 0.2, 0.8)
    first_row = jnp.stack([diagonal[:, 0], crossed[:, 0], depth_terms[:, 0], shifts[:, 0]], axis=1)
    second_row = jnp.stack([crossed[:, 1], diagonal[:, 1], depth_terms[:, 1], shifts[:, 1]], axis=1)
    return jnp.stack([first_row, second_row], axis=1)


def draw_camera(key, part):
    screen_rows = camera_rows(key)
    key = jax.random.fold_in(key, 7)
    depth_row = jax.random.uniform(key, (VIEWS, 1, 4), jnp.float32, -1.0, 1.0)
    return jnp.concatenate([screen_rows, depth_row], axis=1)


def draw_tile_of(key, part):
    blocks = block_orders(key)
    key = jax.random.fold_in(key, 13)
    block_wide, block_high = tiling()
    streams = jax.random.split(key, VIEWS * N_SPACE)
    inner = jax.vmap(lambda stream: jax.random.permutation(stream, TILES_DEV))(streams)
    inner = inner.astype(jnp.int32).reshape(VIEWS, N_SPACE, TILES_DEV)
    across_blocks = 32 // block_wide
    col_tile = (blocks % across_blocks)[:, :, None] * block_wide + inner % block_wide
    row_tile = (blocks // across_blocks)[:, :, None] * block_high + inner // block_wide
    return (row_tile * 32 + col_tile).reshape(VIEWS, SLOTS)


def draw_fetch(key, part):
    orders = owner_orders(key)
    return orders.reshape(N_SPACE, VIEWS, N_SPACE, CAP).transpose(1, 2, 0, 3)


def draw_params(key, part):
    orders = owner_orders(key)
    blocks = block_orders(key)
    screen_rows = camera_rows(key)
    key = jax.random.fold_in(key, 11)
    keys = jax.random.split(key, 8)
    place = jnp.argsort(orders, axis=1).astype(jnp.int32)
    view_ids = place // (N_SPACE * CAP)
    renderer = place // CAP % N_SPACE
    block = blocks[view_ids, renderer]
    block_wide, block_high = tiling()
    across_blocks = 32 // block_wide
    left_edge = (block % across_blocks * (block_wide * 16)).astype(jnp.float32)
    top_edge = (block // across_blocks * (block_high * 16)).astype(jnp.float32)
    spot_x = jax.random.uniform(keys[0], (N_SPACE, G_DEV), jnp.float32, 0.0, 1.0)
    spot_y = jax.random.uniform(keys[1], (N_SPACE, G_DEV), jnp.float32, 0.0, 1.0)
    goal_x = (left_edge - 8.0 + spot_x * float(block_wide * 16 + 16)) / 512.0
    goal_y = (top_edge - 8.0 + spot_y * float(block_high * 16 + 16)) / 512.0
    depth = jax.random.uniform(keys[2], (N_SPACE, G_DEV), jnp.float32, -1.0, 1.0)

    def entry(row, col):
        return screen_rows[:, row, col][view_ids]
    rest_x = goal_x - entry(0, 3) - entry(0, 2) * depth
    rest_y = goal_y - entry(1, 3) - entry(1, 2) * depth
    determinant = entry(0, 0) * entry(1, 1) - entry(0, 1) * entry(1, 0)
    centre_x = (entry(1, 1) * rest_x - entry(0, 1) * rest_y) / determinant
    centre_y = (entry(0, 0) * rest_y - entry(1, 0) * rest_x) / determinant
    centre = jnp.stack([centre_x, centre_y, depth]).reshape(3, G)
    quat_first = jax.random.uniform(keys[3], (1, G), jnp.float32, 1.0, 2.0)
    scales = jax.random.uniform(keys[4], (3, G), jnp.float32, -4.6, -3.0)
    quat_rest = jnp.clip(0.7 * jax.random.normal(keys[5], (3, G), jnp.float32), -2.0, 2.0)
    opacity = jnp.clip(-2.5 + jax.random.normal(keys[6], (1, G), jnp.float32), -6.0, 1.5)
    coeffs = jnp.clip(0.5 * jax.random.normal(keys[7], (48, G), jnp.float32), -2.0, 2.0)
    return jnp.concatenate([centre, scales, quat_first, quat_rest, opacity, coeffs], axis=0)


def draw_lists(key, part):
    key = jax.random.fold_in(key, 37)
    entries = jax.random.randint(key, (VIEWS, SLOTS, K), 0, N_SPACE * CAP, dtype=jnp.int32)
    entries = entries.at[:, 0, 0].set(N_SPACE * CAP - 1)
    return entries.at[:, 0, 1].set(0)


def draw_counts(key, part):
    key = jax.random.fold_in(key, 41)
    loads = jax.random.randint(key, (VIEWS, SLOTS), 1, K + 1, dtype=jnp.int32)
    loads = loads.at[:, 0].set(K)
    return loads.at[:, 1].set(1)


def block_scale(key, dims, shards, least, top_value):
    loudness, own = 1.0, jax.random.fold_in(key, 6)
    for position, blocks in shards:
        heights = jnp.exp(jax.random.uniform(jax.random.fold_in(own, position), (blocks,), jnp.float32, least / len(shards), top_value / len(shards)))
        loudness = loudness * jnp.repeat(heights, dims[position] // blocks).reshape([-1 if axis == position else 1 for axis in range(len(dims))])
    return loudness


def bell_draw(own_key, dims, width, limit, pieces=(), held_as=jnp.bfloat16):
    values = width * jax.random.normal(own_key, dims, jnp.float32)
    if pieces:
        values = values * block_scale(own_key, dims, pieces, -0.22, 0.18)
    return jnp.clip(values, -limit, limit).astype(held_as)


def setup_inputs(seed: int = 0) -> dict:
    streams_of = jax.random.split(jax.random.key(seed), 9)
    return {
        "params": draw_params(jax.random.fold_in(streams_of[8], 71), 0),
        "camera": draw_camera(jax.random.fold_in(streams_of[8], 71), 0),
        "eye_point": bell_draw(streams_of[2], (VIEWS, 3), 3.0, 9.0, ((0, 2),), jnp.float32),
        "tile_of": draw_tile_of(jax.random.fold_in(streams_of[8], 71), 0),
        "fetch": draw_fetch(jax.random.fold_in(streams_of[8], 71), 0),
        "lists": draw_lists(jax.random.fold_in(streams_of[8], 71), 0),
        "counts": draw_counts(jax.random.fold_in(streams_of[8], 71), 0),
        "target": bell_draw(streams_of[7], (VIEWS, SLOTS, 3, 256), 0.3, 2.0, ((0, 2), (1, 64)), jnp.float32),
    }


DILATE = 0.3 / 262144.0
HARM_ZERO = 0.28209479177387814
HARM_ONE = 0.4886025119029199
HARM_TWO = (1.0925484305920792, -1.0925484305920792, 0.31539156525252005, -1.0925484305920792, 0.5462742152960396)
HARM_THREE = (-0.5900435899266435, 2.890611442640554, -0.4570457994644658, 0.3731763325901154, -0.4570457994644658, 1.445305721320277, -0.5900435899266435)

def harmonics(dir_x, dir_y, dir_z):
    sq_x, sq_y, sq_z = (dir_x * dir_x, dir_y * dir_y, dir_z * dir_z)
    return [HARM_ZERO * jnp.ones_like(dir_x), -HARM_ONE * dir_y, HARM_ONE * dir_z, -HARM_ONE * dir_x, HARM_TWO[0] * dir_x * dir_y, HARM_TWO[1] * dir_y * dir_z, HARM_TWO[2] * (2.0 * sq_z - sq_x - sq_y), HARM_TWO[3] * dir_x * dir_z, HARM_TWO[4] * (sq_x - sq_y), HARM_THREE[0] * dir_y * (3.0 * sq_x - sq_y), HARM_THREE[1] * dir_x * dir_y * dir_z, HARM_THREE[2] * dir_y * (4.0 * sq_z - sq_x - sq_y), HARM_THREE[3] * dir_z * (2.0 * sq_z - 3.0 * sq_x - 3.0 * sq_y), HARM_THREE[4] * dir_x * (4.0 * sq_z - sq_x - sq_y), HARM_THREE[5] * dir_z * (sq_x - sq_y), HARM_THREE[6] * dir_x * (sq_x - 3.0 * sq_y)]

def project(params, camera, eye_point):
    centre = params[0:3]
    scales = jnp.exp(params[3:6])
    quat = params[6:10]
    quat = quat / jnp.sqrt(lax.optimization_barrier(jnp.sum(quat * quat, axis=0, keepdims=True)))
    q_w, q_x, q_y, q_z = (quat[0], quat[1], quat[2], quat[3])
    rotation = [[1.0 - 2.0 * (q_y * q_y + q_z * q_z), 2.0 * (q_x * q_y - q_w * q_z), 2.0 * (q_x * q_z + q_w * q_y)], [2.0 * (q_x * q_y + q_w * q_z), 1.0 - 2.0 * (q_x * q_x + q_z * q_z), 2.0 * (q_y * q_z - q_w * q_x)], [2.0 * (q_x * q_z - q_w * q_y), 2.0 * (q_y * q_z + q_w * q_x), 1.0 - 2.0 * (q_x * q_x + q_y * q_y)]]
    jacob = [[(camera[row, 0] * rotation[0][col] + camera[row, 1] * rotation[1][col] + camera[row, 2] * rotation[2][col]) * scales[col] for col in range(3)] for row in range(2)]
    cov_xx = jacob[0][0] * jacob[0][0] + jacob[0][1] * jacob[0][1] + jacob[0][2] * jacob[0][2] + DILATE
    cov_xy = jacob[0][0] * jacob[1][0] + jacob[0][1] * jacob[1][1] + jacob[0][2] * jacob[1][2]
    cov_yy = jacob[1][0] * jacob[1][0] + jacob[1][1] * jacob[1][1] + jacob[1][2] * jacob[1][2] + DILATE
    determinant = cov_xx * cov_yy - cov_xy * cov_xy
    screen_x = camera[0, 0] * centre[0] + camera[0, 1] * centre[1] + camera[0, 2] * centre[2] + camera[0, 3]
    screen_y = camera[1, 0] * centre[0] + camera[1, 1] * centre[1] + camera[1, 2] * centre[2] + camera[1, 3]
    opacity = jax.nn.sigmoid(params[10])
    offset = centre - eye_point[:, None]
    inverse = 1.0 / jnp.sqrt(lax.optimization_barrier(jnp.sum(offset * offset, axis=0)) + 1.0)
    basis = jnp.stack(harmonics(offset[0] * inverse, offset[1] * inverse, offset[2] * inverse))
    coeffs = params[11:59].reshape(16, 3, params.shape[1])
    colour = jnp.maximum(lax.optimization_barrier(jnp.sum(basis[:, None, :] * coeffs, axis=0)) + 0.5, 0.0)
    return jnp.stack([screen_x, screen_y, cov_yy / determinant, -cov_xy / determinant, cov_xx / determinant, opacity, colour[0], colour[1], colour[2]])

def composite(entries, count, tile, cumulate):
    pixel = jnp.arange(256, dtype=jnp.int32)
    col_pix = tile % 32 * 16 + pixel % 16
    row_pix = tile // 32 * 16 + pixel // 16
    pos_x = (col_pix.astype(jnp.float32) + 0.5) / 512.0
    pos_y = (row_pix.astype(jnp.float32) + 0.5) / 512.0
    off_x = pos_x[:, None] - entries[0][None, :]
    off_y = pos_y[:, None] - entries[1][None, :]
    power = -0.5 * (entries[2][None, :] * off_x * off_x + entries[4][None, :] * off_y * off_y) - entries[3][None, :] * off_x * off_y
    alphas = entries[5][None, :] * jnp.exp(power)
    live = jnp.arange(entries.shape[1], dtype=jnp.int32) < count
    alphas = jnp.where(live[None, :], alphas, 0.0)
    before = cumulate(jnp.log1p(-alphas))
    weights = jnp.exp(before) * alphas
    return lax.optimization_barrier(jnp.sum(weights[None, :, :] * entries[6:9][:, None, :], axis=2))

def running_sum(logs):
    summed = jnp.cumsum(logs, axis=1)
    return jnp.concatenate([jnp.zeros_like(logs[:, :1]), summed[:, :-1]], axis=1)

def reference(params, camera, eye_point, tile_of, fetch, lists, counts, target):
    owners = jnp.arange(SLOTS, dtype=jnp.int32) // TILES_DEV
    sources = jnp.arange(N_SPACE, dtype=jnp.int32)[:, None] * G_DEV

    def render_all(values):
        images = []
        for view in range(VIEWS):
            projected = project(values, camera[view], eye_point[view])
            global_ids = (sources[None] + fetch[view]).reshape(N_SPACE, N_SPACE * CAP)
            entry_ids = global_ids[owners[:, None], lists[view]]

            def one_tile(operands):
                ids, count, tile = operands
                return composite(projected[:, ids], count, tile, running_sum)
            images.append(lax.map(jax.checkpoint(one_tile), (entry_ids, counts[view], tile_of[view])))
        return jnp.stack(images)
    rendered, backward = jax.vjp(render_all, params)
    grads, = backward((rendered - target) / 256.0)
    return (rendered, grads)
```

```python
import functools

import jax
import jax.numpy as jnp
from jax import lax
from jax.experimental import pallas as pl
from jax.experimental.pallas import tpu as pltpu
from jax.sharding import PartitionSpec as P

DILATE = 0.3 / 262144.0
HARM_ZERO = 0.28209479177387814
HARM_ONE = 0.4886025119029199
HARM_TWO = (
    1.0925484305920792,
    -1.0925484305920792,
    0.31539156525252005,
    -1.0925484305920792,
    0.5462742152960396,
)
HARM_THREE = (
    -0.5900435899266435,
    2.890611442640554,
    -0.4570457994644658,
    0.3731763325901154,
    -0.4570457994644658,
    1.445305721320277,
    -0.5900435899266435,
)
LOG2E = 1.4426950408889634
MESH = pl.DeviceIdType.MESH
F32 = jnp.float32
BF16 = jnp.bfloat16

N = 64
CAP = 16
TILES = 8
K = 256
PX = 256
ROWS = 59
PITCH = 64
COLS = 16
FEATS = 9
GROUP = 32
MOMS = 16
CHUNK = 32


def harmonics(dir_x, dir_y, dir_z):
    sq_x, sq_y, sq_z = (dir_x * dir_x, dir_y * dir_y, dir_z * dir_z)
    return [
        HARM_ZERO * jnp.ones_like(dir_x),
        -HARM_ONE * dir_y,
        HARM_ONE * dir_z,
        -HARM_ONE * dir_x,
        HARM_TWO[0] * dir_x * dir_y,
        HARM_TWO[1] * dir_y * dir_z,
        HARM_TWO[2] * (2.0 * sq_z - sq_x - sq_y),
        HARM_TWO[3] * dir_x * dir_z,
        HARM_TWO[4] * (sq_x - sq_y),
        HARM_THREE[0] * dir_y * (3.0 * sq_x - sq_y),
        HARM_THREE[1] * dir_x * dir_y * dir_z,
        HARM_THREE[2] * dir_y * (4.0 * sq_z - sq_x - sq_y),
        HARM_THREE[3] * dir_z * (2.0 * sq_z - 3.0 * sq_x - 3.0 * sq_y),
        HARM_THREE[4] * dir_x * (4.0 * sq_z - sq_x - sq_y),
        HARM_THREE[5] * dir_z * (sq_x - sq_y),
        HARM_THREE[6] * dir_x * (sq_x - 3.0 * sq_y),
    ]


def project(rows, camera, eye):
    centre = rows[0:3]
    scales = [jnp.exp(row) for row in rows[3:6]]
    quat = rows[6:10]
    norm = lax.rsqrt(sum(q * q for q in quat))
    q_w, q_x, q_y, q_z = [q * norm for q in quat]
    rotation = [
        [
            1.0 - 2.0 * (q_y * q_y + q_z * q_z),
            2.0 * (q_x * q_y - q_w * q_z),
            2.0 * (q_x * q_z + q_w * q_y),
        ],
        [
            2.0 * (q_x * q_y + q_w * q_z),
            1.0 - 2.0 * (q_x * q_x + q_z * q_z),
            2.0 * (q_y * q_z - q_w * q_x),
        ],
        [
            2.0 * (q_x * q_z - q_w * q_y),
            2.0 * (q_y * q_z + q_w * q_x),
            1.0 - 2.0 * (q_x * q_x + q_y * q_y),
        ],
    ]
    jacob = [
        [
            (
                camera[row][0] * rotation[0][col]
                + camera[row][1] * rotation[1][col]
                + camera[row][2] * rotation[2][col]
            )
            * scales[col]
            for col in range(3)
        ]
        for row in range(2)
    ]
    cov_xx = sum(j * j for j in jacob[0]) + DILATE
    cov_xy = sum(j * i for j, i in zip(jacob[0], jacob[1]))
    cov_yy = sum(j * j for j in jacob[1]) + DILATE
    inv_det = 1.0 / (cov_xx * cov_yy - cov_xy * cov_xy)
    screen = [
        camera[row][0] * centre[0]
        + camera[row][1] * centre[1]
        + camera[row][2] * centre[2]
        + camera[row][3]
        for row in range(2)
    ]
    logit = rows[10]
    log_opacity = jnp.minimum(logit, 0.0) - jnp.log1p(jnp.exp(-jnp.abs(logit)))
    offset = [c - e for c, e in zip(centre, eye)]
    inverse = lax.rsqrt(sum(o * o for o in offset) + 1.0)
    basis = harmonics(*[o * inverse for o in offset])
    colours = [
        jnp.maximum(sum(b * rows[11 + 3 * l + c] for l, b in enumerate(basis)) + 0.5, 0.0)
        for c in range(3)
    ]
    return [
        *screen,
        cov_yy * inv_det,
        -cov_xy * inv_det,
        cov_xx * inv_det,
        log_opacity,
        *colours,
    ]


def split(value, parts):
    pieces = []
    for _ in range(parts - 1):
        piece = value.astype(BF16).astype(F32)
        pieces.append(piece)
        value = value - piece
    return [*pieces, value.astype(BF16).astype(F32)]


def split_low(value, parts):
    pieces = []
    for _ in range(parts - 1):
        piece = value.astype(BF16)
        pieces.append(piece)
        value = value - piece.astype(F32)
    return [*pieces, value.astype(BF16)]


def iota(shape, dim):
    return lax.broadcasted_iota(jnp.int32, shape, dim)


def pick(table, row, lane):
    shape = row.shape
    found = jnp.zeros(shape, F32)
    for r in range(16):
        line = jnp.broadcast_to(table[r : r + 1, :], shape)
        found = jnp.where(row == r, jnp.take_along_axis(line, lane, axis=1), found)
    return found


def dot_nt(left, right):
    return lax.dot_general(left, right, (((1,), (1,)), ((), ())), preferred_element_type=F32)


def render_kernel(
    params_ref,
    cam_ref,
    eye_ref,
    camv_ref,
    eyev_ref,
    tile_ref,
    count_ref,
    fetch_ref,
    lists_ref,
    target_ref,
    rendered_ref,
    dense_ref,
    cams_ref,
    pv,
    pj,
    ask,
    req,
    rowsend,
    rowsin,
    stage,
    stage_hi,
    lhs,
    rhs,
    alphas,
    weights,
    lanes,
    gsend,
    gin,
    turned,
    spare_ask,
    spare_rows,
    spare_grads,
    cam_sem,
    par_sem,
    send_sems,
    recv_sems,
):
    me = lax.axis_index("space")
    view = lax.axis_index("view")
    other = 1 - view

    def blank():
        stage[...] = jnp.zeros(stage.shape, F32)
        stage_hi[...] = jnp.zeros(stage.shape, F32)

    def lay(first, stride, value):
        stage[pl.ds(first, TILES, stride=stride), :] = value[:, 0:128]
        stage_hi[pl.ds(first, TILES, stride=stride), :] = value[:, 128:256]

    def take(first, stride):
        rows = pl.ds(first, TILES, stride=stride)
        return jnp.concatenate([stage[rows, :], stage_hi[rows, :]], axis=1)

    def staged(rows=slice(None)):
        return jnp.concatenate([stage[rows, :], stage_hi[rows, :]], axis=1)

    barrier = pltpu.get_barrier_semaphore()

    def greet_own(d, c):
        pl.semaphore_signal(
            barrier, inc=1, device_id=(lax.rem(me + d, N), view), device_id_type=MESH
        )
        return c

    def greet_other(d, c):
        pl.semaphore_signal(
            barrier, inc=1, device_id=(lax.rem(me + d, N), other), device_id_type=MESH
        )
        return c

    lax.fori_loop(1, N, greet_own, 0)
    lax.fori_loop(0, N, greet_other, 0)

    loads = [
        pltpu.make_async_copy(
            params_ref.at[:, pl.ds(128 * b, 128)], pv.at[pl.ds(PITCH * b, ROWS)], par_sem.at[b]
        )
        for b in range(COLS)
    ]
    for load in loads:
        load.start()
    ask[...] = jnp.zeros(ask.shape, jnp.int32)
    ask[:, 0:CAP] = fetch_ref[...]
    cams_ref[0:8, :] = jnp.zeros((8, 128), F32)
    cams_ref[0:3, 0:4] = camv_ref[...]
    cams_ref[3:4, 0:3] = eyev_ref[...]
    rowsin[...] = jnp.zeros(rowsin.shape, F32)
    pl.semaphore_wait(barrier, 2 * N - 1)

    def push(src, dst, device, sems):
        return pltpu.make_async_remote_copy(
            src_ref=src,
            dst_ref=dst,
            send_sem=send_sems.at[sems],
            recv_sem=recv_sems.at[sems],
            device_id=device,
            device_id_type=MESH,
        )

    def exchange(src, dst, own, sems):
        def one(d, c):
            t = lax.rem(me + d, N)
            push(
                src.at[pl.ds(t, 1)],
                dst.at[pl.ds(me if own else N + me, 1)],
                (t, view if own else other),
                sems,
            ).start()
            return c

        lax.fori_loop(1 if own else 0, N, one, 0)

    def finish_send(src, own, sems):
        push(src, src, (me, view), sems).wait_send()

    def finish_recv(dst, own, sems):
        rows = pl.ds(0, N) if own else pl.ds(N, N)
        push(dst.at[rows], dst.at[rows], (me, view), sems).wait_recv()

    def keep(src, dst, spare, sems):
        mine = src.at[pl.ds(me, 1)]
        pltpu.make_async_copy(mine, dst.at[pl.ds(me, 1)], recv_sems.at[sems]).start()
        pltpu.make_async_copy(mine, spare, send_sems.at[sems]).start()

    exchange(ask, req, True, 0)
    keep(ask, req, spare_ask, 0)
    exchange(ask, req, False, 1)
    greeting = pltpu.make_async_remote_copy(
        src_ref=cams_ref.at[pl.ds(0, 8)],
        dst_ref=cams_ref.at[pl.ds(8, 8)],
        send_sem=cam_sem.at[0],
        recv_sem=cam_sem.at[1],
        device_id=(me, other),
        device_id_type=MESH,
    )
    greeting.start()

    for load in loads:
        load.wait()
    camera = [[cam_ref[r, c] for c in range(4)] for r in range(2)]
    eye = [eye_ref[0, c] for c in range(3)]
    values = [pv[pl.ds(p, COLS, stride=PITCH), :] for p in range(ROWS)]
    for f, row in enumerate(project(values, camera, eye)):
        pj[f] = row

    finish_recv(req, True, 0)
    wanted = jnp.concatenate([req[0:N, :], jnp.zeros((N, 128), jnp.int32)], axis=0).T[0:CAP, :]
    want_row, want_lane = wanted >> 7, wanted & 127

    def collect(f, c):
        stage[pl.ds(pl.multiple_of(f * CAP, CAP), CAP), :] = pick(pj[f], want_row, want_lane)
        return c

    lax.fori_loop(0, FEATS, collect, 0)
    rowsend[...] = stage[...].T[0:N, :]
    exchange(rowsend, rowsin, True, 2)
    keep(rowsend, rowsin, spare_rows, 2)

    finish_recv(req, False, 1)
    turned[...] = req[...].T[0:CAP, :]

    def locate(j, found):
        line = turned[pl.ds(j, 1), :]
        line_hi, line_lo = line >> 7, line & 127
        hit = iota((COLS, 128), 0) == jnp.broadcast_to(line_hi, (COLS, 128))
        spot = iota((COLS, 128), 1).astype(F32)
        digits = jnp.concatenate(
            [
                jnp.where(hit, j.astype(F32), 0.0),
                jnp.where(hit, spot, 0.0),
            ],
            axis=0,
        ).astype(BF16)
        ones = jnp.where(
            iota((128, 128), 0) == jnp.broadcast_to(line_lo, (128, 128)), 1.0, 0.0
        ).astype(BF16)
        return found + dot_nt(digits, ones)

    found = lax.fori_loop(0, CAP, locate, jnp.zeros((2 * COLS, 128), F32))
    found_row = found[0:COLS].astype(jnp.int32)
    found_lane = found[COLS : 2 * COLS].astype(jnp.int32)
    dense_ref[FEATS] = jnp.where(found_lane < N, 1.0, 0.0)

    pixel = iota((TILES, PX), 1)
    u = (pixel % 16).astype(F32) - 7.5
    w = (pixel // 16).astype(F32) - 7.5
    basis = [jnp.ones_like(u), u, w, u * u, u * w, w * w]
    blank()
    for c in range(6):
        for part in range(3):
            lay(3 * c + part, GROUP, basis[c])
    rhs[...] = staged().astype(BF16)

    entry_own = lists_ref[...] >> 4
    entry_pos = lists_ref[...] & 15
    finish_recv(rowsin, True, 2)
    stage[...] = rowsin[...].T

    entries = []
    for f in range(FEATS):
        table = stage[CAP * f : CAP * (f + 1), :]
        entries.append(
            jnp.concatenate(
                [
                    pick(table, entry_pos[:, h : h + 128], entry_own[:, h : h + 128])
                    for h in (0, 128)
                ],
                axis=1,
            )
        )

    tile_row = iota((TILES, PX), 0)
    mid_x = jnp.zeros((TILES, PX), F32)
    mid_y = jnp.zeros((TILES, PX), F32)
    live = jnp.zeros((TILES, PX), jnp.int32)
    for t in range(TILES):
        here = tile_row == t
        mid_x = jnp.where(here, (tile_ref[0, t] % 32 * 16 + 8).astype(F32), mid_x)
        mid_y = jnp.where(here, (tile_ref[0, t] // 32 * 16 + 8).astype(F32), mid_y)
        live = jnp.where(here, count_ref[0, t], live)
    alive = pixel < live
    spot_x = entries[0] * 512.0 - mid_x
    spot_y = entries[1] * 512.0 - mid_y
    con_a, con_b, con_c = [entries[2 + i] * (1.0 / 262144.0) for i in range(3)]
    lin_x = con_a * spot_x + con_b * spot_y
    lin_y = con_c * spot_y + con_b * spot_x
    level = entries[5] - 0.5 * (spot_x * lin_x + spot_y * lin_y)
    coeffs = [level, lin_x, lin_y, -0.5 * con_a, -con_b, -0.5 * con_c]
    blank()
    for c in range(6):
        coeff = jnp.where(alive, coeffs[c] * LOG2E, -1e30 if c == 0 else 0.0)
        for part, piece in enumerate(split(coeff, 3)):
            lay(3 * c + part, GROUP, piece)
    colours = [jnp.where(alive, entries[6 + c], 0.0) for c in range(3)]
    for c in range(3):
        high, low = split(colours[c], 2)
        for part, piece in enumerate((high, high, low)):
            lay(18 + 3 * c + part, GROUP, piece)
        lay(27 + c, GROUP, colours[c])
    lanes[...] = staged().T

    group_mask = iota((TILES, TILES * GROUP), 1) // GROUP == iota((TILES, TILES * GROUP), 0)

    def forward(step, carry):
        through, images = carry[0], list(carry[1:])
        first = pl.multiple_of(step * CHUNK, CHUNK)
        rows = pl.ds(pl.multiple_of(step * CHUNK * TILES, CHUNK * TILES), CHUNK * TILES)
        spread = jnp.where(
            group_mask[None], lanes[pl.ds(first, CHUNK), :][:, None, :], 0.0
        ).reshape(CHUNK * TILES, TILES * GROUP)
        low = spread.astype(BF16)
        lhs[rows, :] = low
        power = jnp.dot(low, rhs[...], preferred_element_type=F32)
        alpha_all = jnp.exp2(power)
        for i in range(CHUNK):
            alpha = alpha_all[i * TILES : (i + 1) * TILES]
            weight = through * alpha
            through = through - weight
            at = pl.ds(pl.multiple_of((first + i) * TILES, TILES), TILES)
            alphas[at, :] = alpha
            weights[at, :] = weight
            group = spread[i * TILES : (i + 1) * TILES]
            for c in range(3):
                line = jnp.sum(
                    jnp.where(iota((TILES, TILES * GROUP), 1) % GROUP == 27 + c, group, 0.0),
                    axis=1,
                    keepdims=True,
                )
                images[c] = images[c] + weight * line
        return (through, *images)

    zero = jnp.zeros((TILES, PX), F32)
    _, *images = lax.fori_loop(0, K // CHUNK, forward, (jnp.ones((TILES, PX), F32), zero, zero, zero))

    blank()
    shades = []
    for c in range(3):
        rendered_ref[:, c, :] = images[c]
        shade = (images[c] - target_ref[:, c, :]) * (1.0 / 256.0)
        high, low = split(shade, 2)
        shades.append(split(shade, 3))
        for part, piece in enumerate((high, low, high)):
            lay(18 + 3 * c + part, GROUP, piece)
    rhs[...] = staged().astype(BF16)
    blank()
    for c in range(6):
        lay(c, MOMS, basis[c])
    for c in range(3):
        for part in range(3):
            lay(128 + 6 + 3 * c + part, MOMS, shades[c][part])
    moment_rows = staged(slice(0, 128)).astype(BF16)
    shade_rows = staged(slice(128, 256)).astype(BF16)
    moment_mask = iota((TILES, 128), 1) // MOMS == iota((TILES, 128), 0)

    def backward(back, behind):
        step = K // CHUNK - 1 - back
        first = pl.multiple_of(step * CHUNK, CHUNK)
        rows = pl.ds(pl.multiple_of(step * CHUNK * TILES, CHUNK * TILES), CHUNK * TILES)
        tone = jnp.dot(lhs[rows, :], rhs[...], preferred_element_type=F32)
        alpha = alphas[rows, :]
        weight = weights[rows, :]
        slopes = [None] * CHUNK
        for i in reversed(range(CHUNK)):
            at = slice(i * TILES, (i + 1) * TILES)
            gap = tone[at] - behind
            slopes[i] = weight[at] * gap
            behind = behind + alpha[at] * gap
        slope = jnp.concatenate(slopes, axis=0)
        total = jnp.zeros((CHUNK * TILES, 128), F32)
        for piece in split_low(slope, 3):
            total = total + dot_nt(piece, moment_rows)
        for piece in split_low(weight, 2):
            total = total + dot_nt(piece, shade_rows)
        total = jnp.where(moment_mask[None], total.reshape(CHUNK, TILES, 128), 0.0)
        lanes[pl.ds(first, CHUNK), 0:128] = jnp.sum(total, axis=1)
        return behind

    lax.fori_loop(0, K // CHUNK, backward, zero)

    turned_sums = lanes[:, 0:128].T
    stage[0:128, :] = turned_sums[:, 0:128]
    stage_hi[0:128, :] = turned_sums[:, 128:256]
    sums = [take(c, MOMS) for c in range(15)]
    s_1, s_u, s_w, s_uu, s_uw, s_ww = sums[0:6]
    d_x = s_u - spot_x * s_1
    d_y = s_w - spot_y * s_1
    d_xx = s_uu - 2.0 * spot_x * s_u + spot_x * spot_x * s_1
    d_yy = s_ww - 2.0 * spot_y * s_w + spot_y * spot_y * s_1
    d_xy = s_uw - spot_x * s_w - spot_y * s_u + spot_x * spot_y * s_1
    slopes = [
        512.0 * (con_a * d_x + con_b * d_y),
        512.0 * (con_c * d_y + con_b * d_x),
        d_xx * (-0.5 / 262144.0),
        d_xy * (-1.0 / 262144.0),
        d_yy * (-0.5 / 262144.0),
        s_1,
        *[sums[6 + 3 * c] + sums[7 + 3 * c] + sums[8 + 3 * c] for c in range(3)],
    ]
    blank()
    for f in range(FEATS):
        for part, piece in enumerate(split(jnp.where(alive, slopes[f], 0.0), 3)):
            lay(FEATS * part + f, GROUP, piece)

    def gather_up(t, total):
        listed = lists_ref[pl.ds(t, 1), :]
        block = staged(pl.ds(pl.multiple_of(t * GROUP, GROUP), GROUP))
        at_pos = iota((CAP, K), 0) == jnp.broadcast_to(listed & 15, (CAP, K))
        left = jnp.where(at_pos[None], block[0 : 3 * FEATS][:, None, :], 0.0)
        left = left.reshape(3 * FEATS * CAP, K).astype(BF16)
        at_own = iota((N, K), 0) == jnp.broadcast_to(listed >> 4, (N, K))
        return total + dot_nt(left, jnp.where(at_own, 1.0, 0.0).astype(BF16))

    total = lax.fori_loop(0, TILES, gather_up, jnp.zeros((3 * FEATS * CAP, N), F32))
    size = FEATS * CAP
    summed = total[0:size] + total[size : 2 * size] + total[2 * size : 3 * size]
    gsend[...] = jnp.zeros(gsend.shape, F32)
    gsend[:, 0:size] = summed.T

    exchange(gsend, gin, True, 3)
    keep(gsend, gin, spare_grads, 3)
    exchange(gsend, gin, False, 4)
    finish_recv(gin, True, 3)
    finish_recv(gin, False, 4)
    stage[...] = gin[...].T

    def place(f, c):
        dense_ref[f] = pick(
            stage[pl.ds(pl.multiple_of(f * CAP, CAP), CAP), :], found_row, found_lane
        )
        return c

    lax.fori_loop(0, FEATS, place, 0)

    finish_send(ask, True, 0)
    finish_send(ask, False, 1)
    finish_send(rowsend, True, 2)
    finish_send(gsend, True, 3)
    finish_send(gsend, False, 4)
    greeting.wait()


def owner_kernel(params_ref, dense_ref, cams_ref, grads_ref, pv, gv, in_sem, out_sem):
    loads = [
        pltpu.make_async_copy(
            params_ref.at[:, pl.ds(128 * b, 128)], pv.at[pl.ds(PITCH * b, ROWS)], in_sem.at[b]
        )
        for b in range(COLS)
    ]
    for load in loads:
        load.start()
    own = dense_ref[FEATS] > 0.5

    def chosen(row, col):
        return jnp.where(
            own,
            jnp.broadcast_to(cams_ref[row : row + 1, col : col + 1], own.shape),
            jnp.broadcast_to(cams_ref[8 + row : 9 + row, col : col + 1], own.shape),
        )

    camera = [[chosen(r, c) for c in range(4)] for r in range(2)]
    eye = [chosen(3, c) for c in range(3)]
    for load in loads:
        load.wait()
    values = [pv[pl.ds(p, COLS, stride=PITCH), :] for p in range(ROWS)]
    _, pull = jax.vjp(lambda rows: project(rows, camera, eye), values)
    (grads,) = pull([dense_ref[f] for f in range(FEATS)])
    for p in range(ROWS):
        gv[pl.ds(p, COLS, stride=PITCH), :] = grads[p]
    stores = [
        pltpu.make_async_copy(
            gv.at[pl.ds(PITCH * b, ROWS)], grads_ref.at[:, pl.ds(128 * b, 128)], out_sem.at[b]
        )
        for b in range(COLS)
    ]
    for store in stores:
        store.start()
    for store in stores:
        store.wait()


def on_device(params, camera, eye_point, tile_of, fetch, lists, counts, target):
    vmem = pl.BlockSpec(memory_space=pltpu.VMEM)
    smem = pl.BlockSpec(memory_space=pltpu.SMEM)
    hbm = pl.BlockSpec(memory_space=pl.ANY)
    rendered, dense, cams = pl.pallas_call(
        render_kernel,
        out_shape=(
            jax.ShapeDtypeStruct((TILES, 3, PX), F32),
            jax.ShapeDtypeStruct((FEATS + 1, COLS, 128), F32),
            jax.ShapeDtypeStruct((16, 128), F32),
        ),
        in_specs=[hbm, smem, smem, vmem, vmem, smem, smem, vmem, vmem, vmem],
        out_specs=(vmem, vmem, vmem),
        scratch_shapes=[
            pltpu.VMEM((COLS * PITCH, 128), F32),
            pltpu.VMEM((FEATS, COLS, 128), F32),
            pltpu.VMEM((N, 128), jnp.int32),
            pltpu.VMEM((2 * N, 128), jnp.int32),
            pltpu.VMEM((N, 256), F32),
            pltpu.VMEM((2 * N, 256), F32),
            pltpu.VMEM((256, 128), F32),
            pltpu.VMEM((256, 128), F32),
            pltpu.VMEM((K * TILES, 256), BF16),
            pltpu.VMEM((256, PX), BF16),
            pltpu.VMEM((K * TILES, PX), F32),
            pltpu.VMEM((K * TILES, PX), F32),
            pltpu.VMEM((K, 256), F32),
            pltpu.VMEM((N, 256), F32),
            pltpu.VMEM((2 * N, 256), F32),
            pltpu.VMEM((CAP, 128), jnp.int32),
            pltpu.VMEM((1, 128), jnp.int32),
            pltpu.VMEM((1, 256), F32),
            pltpu.VMEM((1, 256), F32),
            pltpu.SemaphoreType.DMA((2,)),
            pltpu.SemaphoreType.DMA((COLS,)),
            pltpu.SemaphoreType.DMA((5,)),
            pltpu.SemaphoreType.DMA((5,)),
        ],
        compiler_params=pltpu.CompilerParams(
            collective_id=0, has_side_effects=True, vmem_limit_bytes=40 << 20
        ),
        name="render",
    )(
        params,
        camera[0],
        eye_point,
        camera[0],
        eye_point,
        tile_of,
        counts,
        fetch[0, 0],
        lists[0],
        target[0],
    )
    grads = pl.pallas_call(
        owner_kernel,
        out_shape=jax.ShapeDtypeStruct(params.shape, F32),
        in_specs=[hbm, vmem, vmem],
        out_specs=hbm,
        scratch_shapes=[
            pltpu.VMEM((COLS * PITCH, 128), F32),
            pltpu.VMEM((COLS * PITCH, 128), F32),
            pltpu.SemaphoreType.DMA((COLS,)),
            pltpu.SemaphoreType.DMA((COLS,)),
        ],
        compiler_params=pltpu.CompilerParams(vmem_limit_bytes=32 << 20),
        name="owner",
    )(params, dense, cams)
    return (rendered[None], grads)


def solution(mesh):
    placed = (
        P(None, "space"),
        P("view", None, None),
        P("view", None),
        P("view", "space"),
        P("view", "space", None, None),
        P("view", "space", None),
        P("view", "space"),
        P("view", "space", None, None),
    )
    return jax.shard_map(
        on_device,
        mesh=mesh,
        in_specs=placed,
        out_specs=(P("view", "space", None, None), P(None, "space")),
        check_vma=False,
    )
```

```python
import functools

import jax
import jax.numpy as jnp
from jax import lax
from jax.experimental import pallas as pl
from jax.experimental.pallas import tpu as pltpu
from jax.sharding import PartitionSpec as P

DILATE = 0.3 / 262144.0
HARM_ZERO = 0.28209479177387814
HARM_ONE = 0.4886025119029199
HARM_TWO = (
    1.0925484305920792,
    -1.0925484305920792,
    0.31539156525252005,
    -1.0925484305920792,
    0.5462742152960396,
)
HARM_THREE = (
    -0.5900435899266435,
    2.890611442640554,
    -0.4570457994644658,
    0.3731763325901154,
    -0.4570457994644658,
    1.445305721320277,
    -0.5900435899266435,
)
LOG2E = 1.4426950408889634
MESH = pl.DeviceIdType.MESH
F32 = jnp.float32
BF16 = jnp.bfloat16

N = 64
CAP = 16
TILES = 8
K = 256
PX = 256
ROWS = 59
PITCH = 64
COLS = 16
FEATS = 9
GROUP = 32
MOMS = 16
CHUNK = 32
UNROLL_F = 8
UNROLL_B = 8


def harmonics(dir_x, dir_y, dir_z):
    sq_x, sq_y, sq_z = (dir_x * dir_x, dir_y * dir_y, dir_z * dir_z)
    return [
        HARM_ZERO * jnp.ones_like(dir_x),
        -HARM_ONE * dir_y,
        HARM_ONE * dir_z,
        -HARM_ONE * dir_x,
        HARM_TWO[0] * dir_x * dir_y,
        HARM_TWO[1] * dir_y * dir_z,
        HARM_TWO[2] * (2.0 * sq_z - sq_x - sq_y),
        HARM_TWO[3] * dir_x * dir_z,
        HARM_TWO[4] * (sq_x - sq_y),
        HARM_THREE[0] * dir_y * (3.0 * sq_x - sq_y),
        HARM_THREE[1] * dir_x * dir_y * dir_z,
        HARM_THREE[2] * dir_y * (4.0 * sq_z - sq_x - sq_y),
        HARM_THREE[3] * dir_z * (2.0 * sq_z - 3.0 * sq_x - 3.0 * sq_y),
        HARM_THREE[4] * dir_x * (4.0 * sq_z - sq_x - sq_y),
        HARM_THREE[5] * dir_z * (sq_x - sq_y),
        HARM_THREE[6] * dir_x * (sq_x - 3.0 * sq_y),
    ]


def project(rows, camera, eye):
    centre = rows[0:3]
    scales = [jnp.exp(row) for row in rows[3:6]]
    quat = rows[6:10]
    norm = lax.rsqrt(sum(q * q for q in quat))
    q_w, q_x, q_y, q_z = [q * norm for q in quat]
    rotation = [
        [
            1.0 - 2.0 * (q_y * q_y + q_z * q_z),
            2.0 * (q_x * q_y - q_w * q_z),
            2.0 * (q_x * q_z + q_w * q_y),
        ],
        [
            2.0 * (q_x * q_y + q_w * q_z),
            1.0 - 2.0 * (q_x * q_x + q_z * q_z),
            2.0 * (q_y * q_z - q_w * q_x),
        ],
        [
            2.0 * (q_x * q_z - q_w * q_y),
            2.0 * (q_y * q_z + q_w * q_x),
            1.0 - 2.0 * (q_x * q_x + q_y * q_y),
        ],
    ]
    jacob = [
        [
            (
                camera[row][0] * rotation[0][col]
                + camera[row][1] * rotation[1][col]
                + camera[row][2] * rotation[2][col]
            )
            * scales[col]
            for col in range(3)
        ]
        for row in range(2)
    ]
    cov_xx = sum(j * j for j in jacob[0]) + DILATE
    cov_xy = sum(j * i for j, i in zip(jacob[0], jacob[1]))
    cov_yy = sum(j * j for j in jacob[1]) + DILATE
    inv_det = 1.0 / (cov_xx * cov_yy - cov_xy * cov_xy)
    screen = [
        camera[row][0] * centre[0]
        + camera[row][1] * centre[1]
        + camera[row][2] * centre[2]
        + camera[row][3]
        for row in range(2)
    ]
    logit = rows[10]
    log_opacity = jnp.minimum(logit, 0.0) - jnp.log1p(jnp.exp(-jnp.abs(logit)))
    offset = [c - e for c, e in zip(centre, eye)]
    inverse = lax.rsqrt(sum(o * o for o in offset) + 1.0)
    basis = harmonics(*[o * inverse for o in offset])
    colours = [
        jnp.maximum(sum(b * rows[11 + 3 * l + c] for l, b in enumerate(basis)) + 0.5, 0.0)
        for c in range(3)
    ]
    return [
        *screen,
        cov_yy * inv_det,
        -cov_xy * inv_det,
        cov_xx * inv_det,
        log_opacity,
        *colours,
    ]


def split(value, parts):
    pieces = []
    for _ in range(parts - 1):
        piece = value.astype(BF16).astype(F32)
        pieces.append(piece)
        value = value - piece
    return [*pieces, value.astype(BF16).astype(F32)]


def split_low(value, parts):
    pieces = []
    for _ in range(parts - 1):
        piece = value.astype(BF16)
        pieces.append(piece)
        value = value - piece.astype(F32)
    return [*pieces, value.astype(BF16)]


def iota(shape, dim):
    return lax.broadcasted_iota(jnp.int32, shape, dim)


def pick(table, row, lane):
    shape = row.shape
    found = jnp.zeros(shape, F32)
    for r in range(table.shape[0]):
        line = jnp.broadcast_to(table[r : r + 1, :], shape)
        found = jnp.where(row == r, jnp.take_along_axis(line, lane, axis=1), found)
    return found


def dot_nt(left, right):
    return lax.dot_general(left, right, (((1,), (1,)), ((), ())), preferred_element_type=F32)


def render_kernel(
    params_hbm,
    cam_hbm,
    eye_hbm,
    tile_hbm,
    count_hbm,
    fetch_hbm,
    lists_hbm,
    target_hbm,
    rendered_ref,
    dense_ref,
    cams_ref,
    cam_ref,
    eye_ref,
    tile_ref,
    count_ref,
    fetch_ref,
    lists_ref,
    target_ref,
    pv,
    pj,
    ask,
    req,
    rowsend,
    rowsin,
    stage,
    stage_hi,
    lhs,
    rhs,
    alphas,
    weights,
    lanes,
    gsend,
    gin,
    turned,
    spare_ask,
    spare_rows,
    spare_grads,
    pos_ones,
    own_ones,
    in_sems,
    cam_sem,
    par_sem,
    send_sems,
    recv_sems,
):
    me = lax.axis_index("space")
    view = lax.axis_index("view")
    other = 1 - view

    def blank():
        stage[...] = jnp.zeros(stage.shape, F32)
        stage_hi[...] = jnp.zeros(stage.shape, F32)

    def lay(first, stride, value):
        stage[pl.ds(first, TILES, stride=stride), :] = value[:, 0:128]
        stage_hi[pl.ds(first, TILES, stride=stride), :] = value[:, 128:256]

    def take(first, stride):
        rows = pl.ds(first, TILES, stride=stride)
        return jnp.concatenate([stage[rows, :], stage_hi[rows, :]], axis=1)

    def staged(rows=slice(None)):
        return jnp.concatenate([stage[rows, :], stage_hi[rows, :]], axis=1)

    small = [
        pltpu.make_async_copy(src, dst, in_sems.at[i])
        for i, (src, dst) in enumerate(
            [
                (fetch_hbm, fetch_ref),
                (cam_hbm, cam_ref),
                (eye_hbm, eye_ref),
                (tile_hbm, tile_ref),
                (count_hbm, count_ref),
                (lists_hbm, lists_ref),
                (target_hbm, target_ref),
            ]
        )
    ]
    small[0].start()
    barrier = pltpu.get_barrier_semaphore()
    pl.semaphore_signal(barrier, inc=1, device_id=(me, other), device_id_type=MESH)

    def greet(d, c):
        pl.semaphore_signal(
            barrier, inc=1, device_id=(lax.rem(me + d, N), view), device_id_type=MESH
        )
        return c

    lax.fori_loop(1, N, greet, 0, unroll=7)
    loads = [
        pltpu.make_async_copy(
            params_hbm.at[:, pl.ds(128 * b, 128)], pv.at[pl.ds(PITCH * b, ROWS)], par_sem.at[b]
        )
        for b in range(COLS)
    ]
    for load in [*small[1:], *loads]:
        load.start()
    ask[...] = jnp.zeros(ask.shape, jnp.int32)
    rowsin[...] = jnp.zeros(rowsin.shape, F32)
    small[0].wait()
    ask[:, 0:CAP] = fetch_ref[...].T
    pl.semaphore_wait(barrier, N)

    def push(src, dst, device, sems):
        return pltpu.make_async_remote_copy(
            src_ref=src,
            dst_ref=dst,
            send_sem=send_sems.at[sems],
            recv_sem=recv_sems.at[sems],
            device_id=device,
            device_id_type=MESH,
        )

    def exchange(src, dst, own, sems):
        def one(d, c):
            t = lax.rem(me + d, N)
            push(
                src.at[pl.ds(t, 1)],
                dst.at[pl.ds(me if own else N + me, 1)],
                (t, view if own else other),
                sems,
            ).start()
            return c

        lax.fori_loop(1 if own else 0, N, one, 0, unroll=7 if own else 8)

    def finish_send(src, own, sems):
        push(src, src, (me, view), sems).wait_send()

    def finish_recv(dst, own, sems):
        rows = pl.ds(0, N) if own else pl.ds(N, N)
        push(dst.at[rows], dst.at[rows], (me, view), sems).wait_recv()

    def keep(src, dst, spare, sems):
        mine = src.at[pl.ds(me, 1)]
        pltpu.make_async_copy(mine, dst.at[pl.ds(me, 1)], recv_sems.at[sems]).start()
        pltpu.make_async_copy(mine, spare, send_sems.at[sems]).start()

    exchange(ask, req, True, 0)
    keep(ask, req, spare_ask, 0)
    for load in [*small[1:], *loads]:
        load.wait()
    camera = [[cam_ref[r, 0, c] for c in range(4)] for r in range(2)]
    eye = [eye_ref[0, c] for c in range(3)]
    values = [pv[pl.ds(p, COLS, stride=PITCH), :] for p in range(ROWS)]
    for f, row in enumerate(project(values, camera, eye)):
        pj[f] = row

    sheet = jnp.zeros((8, 128), F32)
    spots = [(r, c, camera[r][c]) for r in range(2) for c in range(4)]
    spots += [(3, c, eye[c]) for c in range(3)]
    for r, c, number in spots:
        here = (iota((8, 128), 0) == r) & (iota((8, 128), 1) == c)
        sheet = jnp.where(here, number, sheet)
    cams_ref[0:8, :] = sheet
    greeting = pltpu.make_async_remote_copy(
        src_ref=cams_ref.at[pl.ds(0, 8)],
        dst_ref=cams_ref.at[pl.ds(8, 8)],
        send_sem=cam_sem.at[0],
        recv_sem=cam_sem.at[1],
        device_id=(me, other),
        device_id_type=MESH,
    )
    greeting.start()

    finish_recv(req, True, 0)
    wanted = req[0:N, :].T[0:CAP, :]
    wanted = jnp.concatenate([wanted[0:8], wanted[8:16]], axis=1)
    want_row, want_lane = wanted >> 7, wanted & 127
    for f in range(FEATS):
        found = pick(pj[f], want_row, want_lane)
        stage[CAP * f : CAP * f + 8, :] = found
        stage[CAP * f + 8 : CAP * (f + 1), :] = pltpu.roll(found, N, 1)
    rowsend[...] = stage[...].T[0:N, :]
    exchange(rowsend, rowsin, True, 2)
    keep(rowsend, rowsin, spare_rows, 2)

    passed = pltpu.make_async_remote_copy(
        src_ref=req.at[pl.ds(0, N)],
        dst_ref=req.at[pl.ds(N, N)],
        send_sem=send_sems.at[1],
        recv_sem=recv_sems.at[1],
        device_id=(me, other),
        device_id_type=MESH,
    )
    passed.start()

    passed.wait_recv()
    turned[...] = req[...].T[0:CAP, :]

    def locate(j, found):
        line = turned[pl.ds(j, 1), :]
        line_hi, line_lo = line >> 7, line & 127
        hit = iota((COLS, 128), 0) == jnp.broadcast_to(line_hi, (COLS, 128))
        spot = iota((COLS, 128), 1).astype(F32)
        digits = jnp.concatenate(
            [
                jnp.where(hit, j.astype(F32), 0.0),
                jnp.where(hit, spot, 0.0),
            ],
            axis=0,
        ).astype(BF16)
        ones = jnp.where(
            iota((128, 128), 0) == jnp.broadcast_to(line_lo, (128, 128)), 1.0, 0.0
        ).astype(BF16)
        return found + dot_nt(digits, ones)

    found = lax.fori_loop(0, CAP, locate, jnp.zeros((2 * COLS, 128), F32))
    found_row = found[0:COLS].astype(jnp.int32)
    found_lane = found[COLS : 2 * COLS].astype(jnp.int32)
    dense_ref[FEATS] = jnp.where(found_lane < N, 1.0, 0.0)

    pixel = iota((TILES, PX), 1)
    u = (pixel % 16).astype(F32) - 7.5
    w = (pixel // 16).astype(F32) - 7.5
    basis = [jnp.ones_like(u), u, w, u * u, u * w, w * w]
    blank()
    for c in range(6):
        for part in range(3):
            lay(3 * c + part, GROUP, basis[c])
    rhs[...] = staged().astype(BF16)

    for t in range(TILES):
        listed = lists_ref[t : t + 1, :]
        at_pos = iota((CAP, K), 0) == jnp.broadcast_to(listed & 15, (CAP, K))
        at_own = iota((N, K), 0) == jnp.broadcast_to(listed >> 4, (N, K))
        pos_ones[t] = jnp.where(at_pos, 1.0, 0.0).astype(BF16)
        own_ones[t] = jnp.where(at_own, 1.0, 0.0).astype(BF16)

    entry_row = lists_ref[...] & 7
    entry_lane = (lists_ref[...] >> 4) + ((lists_ref[...] & 8) << 3)
    finish_recv(rowsin, True, 2)
    stage[...] = rowsin[...].T

    entries = []
    for f in range(FEATS):
        first_half = stage[CAP * f : CAP * f + 8, :]
        second_half = stage[CAP * f + 8 : CAP * (f + 1), :]
        table = jnp.where(iota((8, 128), 1) < N, first_half, pltpu.roll(second_half, N, 1))
        entries.append(
            jnp.concatenate(
                [
                    pick(table, entry_row[:, h : h + 128], entry_lane[:, h : h + 128])
                    for h in (0, 128)
                ],
                axis=1,
            )
        )

    tile_row = iota((TILES, PX), 0)
    mid_x = jnp.zeros((TILES, PX), F32)
    mid_y = jnp.zeros((TILES, PX), F32)
    live = jnp.zeros((TILES, PX), jnp.int32)
    for t in range(TILES):
        here = tile_row == t
        mid_x = jnp.where(here, (tile_ref[0, t] % 32 * 16 + 8).astype(F32), mid_x)
        mid_y = jnp.where(here, (tile_ref[0, t] // 32 * 16 + 8).astype(F32), mid_y)
        live = jnp.where(here, count_ref[0, t], live)
    alive = pixel < live
    spot_x = entries[0] * 512.0 - mid_x
    spot_y = entries[1] * 512.0 - mid_y
    con_a, con_b, con_c = [entries[2 + i] * (1.0 / 262144.0) for i in range(3)]
    lin_x = con_a * spot_x + con_b * spot_y
    lin_y = con_c * spot_y + con_b * spot_x
    level = entries[5] - 0.5 * (spot_x * lin_x + spot_y * lin_y)
    coeffs = [level, lin_x, lin_y, -0.5 * con_a, -con_b, -0.5 * con_c]
    blank()
    for c in range(6):
        coeff = jnp.where(alive, coeffs[c] * LOG2E, -1e30 if c == 0 else 0.0)
        for part, piece in enumerate(split(coeff, 3)):
            lay(3 * c + part, GROUP, piece)
    colours = [jnp.where(alive, entries[6 + c], 0.0) for c in range(3)]
    for c in range(3):
        high, low, rest = split(colours[c], 3)
        for part, piece in enumerate((high, high, low)):
            lay(18 + 3 * c + part, GROUP, piece)
        lay(27 + c, GROUP, rest)
    lanes[...] = staged().T

    column = iota((TILES * GROUP, 128), 0) % GROUP
    wants = iota((TILES * GROUP, 128), 1)
    adds = (column == 18 + 3 * wants) | (column == 20 + 3 * wants) | (column == 27 + wants)
    chooser = jnp.where(adds & (wants < 3), 1.0, 0.0).astype(BF16)
    group_mask = iota((TILES, TILES * GROUP), 1) // GROUP == iota((TILES, TILES * GROUP), 0)

    def forward(step, carry):
        through, images = carry[0], list(carry[1:])
        first = pl.multiple_of(step * CHUNK, CHUNK)
        rows = pl.ds(pl.multiple_of(step * CHUNK * TILES, CHUNK * TILES), CHUNK * TILES)
        spread = jnp.where(
            group_mask[None], lanes[pl.ds(first, CHUNK), :][:, None, :], 0.0
        ).reshape(CHUNK * TILES, TILES * GROUP)
        low = spread.astype(BF16)
        lhs[rows, :] = low
        power = jnp.dot(low, rhs[...], preferred_element_type=F32)
        paint = jnp.dot(low, chooser, preferred_element_type=F32)
        alpha_all = jnp.exp2(power)
        alphas[rows, :] = alpha_all
        for i in range(CHUNK):
            alpha = alpha_all[i * TILES : (i + 1) * TILES]
            weight = through * alpha
            through = through * (1.0 - alpha)
            at = pl.ds(pl.multiple_of((first + i) * TILES, TILES), TILES)
            weights[at, :] = weight
            for c in range(3):
                shine = paint[i * TILES : (i + 1) * TILES, c : c + 1]
                images[c] = images[c] + weight * shine
        return (through, *images)

    zero = jnp.zeros((TILES, PX), F32)
    _, *images = lax.fori_loop(0, K // CHUNK, forward, (jnp.ones((TILES, PX), F32), zero, zero, zero), unroll=UNROLL_F)

    blank()
    shades = []
    for c in range(3):
        rendered_ref[c] = images[c]
        shade = (images[c] - target_ref[c]) * (1.0 / 256.0)
        high, low = split(shade, 2)
        shades.append(split(shade, 3))
        for part, piece in enumerate((high, low, high)):
            lay(18 + 3 * c + part, GROUP, piece)
    rhs[...] = staged().astype(BF16)
    blank()
    for c in range(6):
        lay(c, MOMS, basis[c])
    for c in range(3):
        for part in range(3):
            lay(128 + 6 + 3 * c + part, MOMS, shades[c][part])
    moment_rows = staged(slice(0, 128)).astype(BF16)
    shade_rows = staged(slice(128, 256)).astype(BF16)
    moment_mask = iota((TILES, 128), 1) // MOMS == iota((TILES, 128), 0)

    def backward(back, behind):
        step = K // CHUNK - 1 - back
        first = pl.multiple_of(step * CHUNK, CHUNK)
        rows = pl.ds(pl.multiple_of(step * CHUNK * TILES, CHUNK * TILES), CHUNK * TILES)
        tone = jnp.dot(lhs[rows, :], rhs[...], preferred_element_type=F32)
        alpha = alphas[rows, :]
        weight = weights[rows, :]
        slopes = [None] * CHUNK
        for i in reversed(range(CHUNK)):
            at = slice(i * TILES, (i + 1) * TILES)
            gap = tone[at] - behind
            slopes[i] = weight[at] * gap
            behind = behind * (1.0 - alpha[at]) + alpha[at] * tone[at]
        slope = jnp.concatenate(slopes, axis=0)
        total = jnp.zeros((CHUNK * TILES, 128), F32)
        for piece in split_low(slope, 2):
            total = total + dot_nt(piece, moment_rows)
        for piece in split_low(weight, 2):
            total = total + dot_nt(piece, shade_rows)
        total = jnp.where(moment_mask[None], total.reshape(CHUNK, TILES, 128), 0.0)
        lanes[pl.ds(first, CHUNK), 0:128] = jnp.sum(total, axis=1)
        return behind

    lax.fori_loop(0, K // CHUNK, backward, zero, unroll=UNROLL_B)

    turned_sums = lanes[:, 0:128].T
    stage[0:128, :] = turned_sums[:, 0:128]
    stage_hi[0:128, :] = turned_sums[:, 128:256]
    sums = [take(c, MOMS) for c in range(15)]
    s_1, s_u, s_w, s_uu, s_uw, s_ww = sums[0:6]
    d_x = s_u - spot_x * s_1
    d_y = s_w - spot_y * s_1
    d_xx = s_uu - 2.0 * spot_x * s_u + spot_x * spot_x * s_1
    d_yy = s_ww - 2.0 * spot_y * s_w + spot_y * spot_y * s_1
    d_xy = s_uw - spot_x * s_w - spot_y * s_u + spot_x * spot_y * s_1
    slopes = [
        512.0 * (con_a * d_x + con_b * d_y),
        512.0 * (con_c * d_y + con_b * d_x),
        d_xx * (-0.5 / 262144.0),
        d_xy * (-1.0 / 262144.0),
        d_yy * (-0.5 / 262144.0),
        s_1,
        *[sums[6 + 3 * c] + sums[7 + 3 * c] + sums[8 + 3 * c] for c in range(3)],
    ]
    blank()
    for f in range(FEATS):
        for part, piece in enumerate(split(jnp.where(alive, slopes[f], 0.0), 2)):
            lay(FEATS * part + f, GROUP, piece)

    total = jnp.zeros((2 * FEATS * CAP, N), F32)
    for t in range(TILES):
        block = staged(slice(t * GROUP, t * GROUP + 2 * FEATS)).astype(BF16)
        left = block[:, None, :] * pos_ones[t][None]
        total = total + dot_nt(left.reshape(2 * FEATS * CAP, K), own_ones[t])
    size = FEATS * CAP
    summed = total[0:size] + total[size : 2 * size]
    gsend[...] = jnp.zeros(gsend.shape, F32)
    gsend[:, 0:size] = summed.T

    exchange(gsend, gin, True, 3)
    keep(gsend, gin, spare_grads, 3)
    exchange(gsend, gin, False, 4)
    finish_recv(gin, True, 3)
    finish_recv(gin, False, 4)
    stage[...] = gin[...].T

    for f in range(FEATS):
        dense_ref[f] = pick(stage[CAP * f : CAP * (f + 1), :], found_row, found_lane)

    finish_send(ask, True, 0)
    passed.wait_send()
    finish_send(rowsend, True, 2)
    finish_send(gsend, True, 3)
    finish_send(gsend, False, 4)
    greeting.wait()


def owner_kernel(
    params_ref, dense_ref, cams_ref, image_ref, grads_ref, rendered_ref, pv, gv, in_sem, out_sem
):
    rendered_ref[...] = image_ref[...]
    loads = [
        pltpu.make_async_copy(
            params_ref.at[:, pl.ds(128 * b, 128)], pv.at[pl.ds(PITCH * b, ROWS)], in_sem.at[b]
        )
        for b in range(COLS)
    ]
    for load in loads:
        load.start()
    own = dense_ref[FEATS] > 0.5

    def chosen(row, col):
        return jnp.where(
            own,
            jnp.broadcast_to(cams_ref[row : row + 1, col : col + 1], own.shape),
            jnp.broadcast_to(cams_ref[8 + row : 9 + row, col : col + 1], own.shape),
        )

    camera = [[chosen(r, c) for c in range(4)] for r in range(2)]
    eye = [chosen(3, c) for c in range(3)]
    for load in loads:
        load.wait()
    values = [pv[pl.ds(p, COLS, stride=PITCH), :] for p in range(ROWS)]
    _, pull = jax.vjp(lambda rows: project(rows, camera, eye), values)
    (grads,) = pull([dense_ref[f] for f in range(FEATS)])
    for p in range(ROWS):
        gv[pl.ds(p, COLS, stride=PITCH), :] = grads[p]
    stores = [
        pltpu.make_async_copy(
            gv.at[pl.ds(PITCH * b, ROWS)], grads_ref.at[:, pl.ds(128 * b, 128)], out_sem.at[b]
        )
        for b in range(COLS)
    ]
    for store in stores:
        store.start()
    for store in stores:
        store.wait()


def on_device(params, camera, eye_point, tile_of, fetch, lists, counts, target):
    vmem = pl.BlockSpec(memory_space=pltpu.VMEM)
    hbm = pl.BlockSpec(memory_space=pltpu.HBM)
    image, dense, cams = pl.pallas_call(
        render_kernel,
        out_shape=(
            jax.ShapeDtypeStruct((3, TILES, PX), F32),
            jax.ShapeDtypeStruct((FEATS + 1, COLS, 128), F32),
            jax.ShapeDtypeStruct((16, 128), F32),
        ),
        in_specs=[hbm] * 8,
        out_specs=(vmem, vmem, vmem),
        scratch_shapes=[
            pltpu.SMEM((3, 1, 4), F32),
            pltpu.SMEM((1, 3), F32),
            pltpu.SMEM((1, TILES), jnp.int32),
            pltpu.SMEM((1, TILES), jnp.int32),
            pltpu.VMEM((CAP, N), jnp.int32),
            pltpu.VMEM((TILES, K), jnp.int32),
            pltpu.VMEM((3, TILES, PX), F32),
            pltpu.VMEM((COLS * PITCH, 128), F32),
            pltpu.VMEM((FEATS, COLS, 128), F32),
            pltpu.VMEM((N, 128), jnp.int32),
            pltpu.VMEM((2 * N, 128), jnp.int32),
            pltpu.VMEM((N, 256), F32),
            pltpu.VMEM((2 * N, 256), F32),
            pltpu.VMEM((256, 128), F32),
            pltpu.VMEM((256, 128), F32),
            pltpu.VMEM((K * TILES, 256), BF16),
            pltpu.VMEM((256, PX), BF16),
            pltpu.VMEM((K * TILES, PX), F32),
            pltpu.VMEM((K * TILES, PX), F32),
            pltpu.VMEM((K, 256), F32),
            pltpu.VMEM((N, 256), F32),
            pltpu.VMEM((2 * N, 256), F32),
            pltpu.VMEM((CAP, 128), jnp.int32),
            pltpu.VMEM((1, 128), jnp.int32),
            pltpu.VMEM((1, 256), F32),
            pltpu.VMEM((1, 256), F32),
            pltpu.VMEM((TILES, CAP, K), BF16),
            pltpu.VMEM((TILES, N, K), BF16),
            pltpu.SemaphoreType.DMA((7,)),
            pltpu.SemaphoreType.DMA((2,)),
            pltpu.SemaphoreType.DMA((COLS,)),
            pltpu.SemaphoreType.DMA((5,)),
            pltpu.SemaphoreType.DMA((5,)),
        ],
        compiler_params=pltpu.CompilerParams(
            collective_id=0, has_side_effects=True, vmem_limit_bytes=56 << 20
        ),
        name="render",
    )(
        params,
        camera.transpose(1, 0, 2),
        eye_point,
        tile_of,
        counts,
        fetch[0, 0].T,
        lists[0],
        target[0].transpose(1, 0, 2),
    )
    grads, rendered = pl.pallas_call(
        owner_kernel,
        out_shape=(
            jax.ShapeDtypeStruct(params.shape, F32),
            jax.ShapeDtypeStruct(image.shape, F32),
        ),
        in_specs=[hbm, vmem, vmem, vmem],
        out_specs=(hbm, vmem),
        scratch_shapes=[
            pltpu.VMEM((COLS * PITCH, 128), F32),
            pltpu.VMEM((COLS * PITCH, 128), F32),
            pltpu.SemaphoreType.DMA((COLS,)),
            pltpu.SemaphoreType.DMA((COLS,)),
        ],
        compiler_params=pltpu.CompilerParams(vmem_limit_bytes=56 << 20),
        name="owner",
    )(params, dense, cams, image)
    return (rendered.transpose(1, 0, 2)[None], grads)


def solution(mesh):
    placed = (
        P(None, "space"),
        P("view", None, None),
        P("view", None),
        P("view", "space"),
        P("view", "space", None, None),
        P("view", "space", None),
        P("view", "space"),
        P("view", "space", None, None),
    )
    return jax.shard_map(
        on_device,
        mesh=mesh,
        in_specs=placed,
        out_specs=(P("view", "space", None, None), P(None, "space")),
        check_vma=False,
    )
```

```python
import functools

import jax
import jax.numpy as jnp
from jax import lax
from jax.experimental import pallas as pl
from jax.experimental.pallas import tpu as pltpu
from jax.sharding import PartitionSpec as P

DILATE = 0.3 / 262144.0
HARM_ZERO = 0.28209479177387814
HARM_ONE = 0.4886025119029199
HARM_TWO = (
    1.0925484305920792,
    -1.0925484305920792,
    0.31539156525252005,
    -1.0925484305920792,
    0.5462742152960396,
)
HARM_THREE = (
    -0.5900435899266435,
    2.890611442640554,
    -0.4570457994644658,
    0.3731763325901154,
    -0.4570457994644658,
    1.445305721320277,
    -0.5900435899266435,
)
LOG2E = 1.4426950408889634
MESH = pl.DeviceIdType.MESH
F32 = jnp.float32
BF16 = jnp.bfloat16

N = 64
CAP = 16
TILES = 8
K = 256
PX = 256
ROWS = 59
PITCH = 64
COLS = 16
FEATS = 9
GROUP = 32
MOMS = 16
CHUNK = 32
UNROLL_F = 8
UNROLL_B = 8


def harmonics(dir_x, dir_y, dir_z):
    sq_x, sq_y, sq_z = (dir_x * dir_x, dir_y * dir_y, dir_z * dir_z)
    return [
        HARM_ZERO * jnp.ones_like(dir_x),
        -HARM_ONE * dir_y,
        HARM_ONE * dir_z,
        -HARM_ONE * dir_x,
        HARM_TWO[0] * dir_x * dir_y,
        HARM_TWO[1] * dir_y * dir_z,
        HARM_TWO[2] * (2.0 * sq_z - sq_x - sq_y),
        HARM_TWO[3] * dir_x * dir_z,
        HARM_TWO[4] * (sq_x - sq_y),
        HARM_THREE[0] * dir_y * (3.0 * sq_x - sq_y),
        HARM_THREE[1] * dir_x * dir_y * dir_z,
        HARM_THREE[2] * dir_y * (4.0 * sq_z - sq_x - sq_y),
        HARM_THREE[3] * dir_z * (2.0 * sq_z - 3.0 * sq_x - 3.0 * sq_y),
        HARM_THREE[4] * dir_x * (4.0 * sq_z - sq_x - sq_y),
        HARM_THREE[5] * dir_z * (sq_x - sq_y),
        HARM_THREE[6] * dir_x * (sq_x - 3.0 * sq_y),
    ]


def project(rows, camera, eye):
    centre = rows[0:3]
    scales = [jnp.exp(row) for row in rows[3:6]]
    quat = rows[6:10]
    norm = lax.rsqrt(sum(q * q for q in quat))
    q_w, q_x, q_y, q_z = [q * norm for q in quat]
    rotation = [
        [
            1.0 - 2.0 * (q_y * q_y + q_z * q_z),
            2.0 * (q_x * q_y - q_w * q_z),
            2.0 * (q_x * q_z + q_w * q_y),
        ],
        [
            2.0 * (q_x * q_y + q_w * q_z),
            1.0 - 2.0 * (q_x * q_x + q_z * q_z),
            2.0 * (q_y * q_z - q_w * q_x),
        ],
        [
            2.0 * (q_x * q_z - q_w * q_y),
            2.0 * (q_y * q_z + q_w * q_x),
            1.0 - 2.0 * (q_x * q_x + q_y * q_y),
        ],
    ]
    jacob = [
        [
            (
                camera[row][0] * rotation[0][col]
                + camera[row][1] * rotation[1][col]
                + camera[row][2] * rotation[2][col]
            )
            * scales[col]
            for col in range(3)
        ]
        for row in range(2)
    ]
    cov_xx = sum(j * j for j in jacob[0]) + DILATE
    cov_xy = sum(j * i for j, i in zip(jacob[0], jacob[1]))
    cov_yy = sum(j * j for j in jacob[1]) + DILATE
    inv_det = 1.0 / (cov_xx * cov_yy - cov_xy * cov_xy)
    screen = [
        camera[row][0] * centre[0]
        + camera[row][1] * centre[1]
        + camera[row][2] * centre[2]
        + camera[row][3]
        for row in range(2)
    ]
    logit = rows[10]
    log_opacity = jnp.minimum(logit, 0.0) - jnp.log1p(jnp.exp(-jnp.abs(logit)))
    offset = [c - e for c, e in zip(centre, eye)]
    inverse = lax.rsqrt(sum(o * o for o in offset) + 1.0)
    basis = harmonics(*[o * inverse for o in offset])
    colours = [
        jnp.maximum(sum(b * rows[11 + 3 * l + c] for l, b in enumerate(basis)) + 0.5, 0.0)
        for c in range(3)
    ]
    return [
        *screen,
        cov_yy * inv_det,
        -cov_xy * inv_det,
        cov_xx * inv_det,
        log_opacity,
        *colours,
    ]


def split(value, parts):
    pieces = []
    for _ in range(parts - 1):
        piece = value.astype(BF16).astype(F32)
        pieces.append(piece)
        value = value - piece
    return [*pieces, value.astype(BF16).astype(F32)]


def split_low(value, parts):
    pieces = []
    for _ in range(parts - 1):
        piece = value.astype(BF16)
        pieces.append(piece)
        value = value - piece.astype(F32)
    return [*pieces, value.astype(BF16)]


def iota(shape, dim):
    return lax.broadcasted_iota(jnp.int32, shape, dim)


def pick(table, row, lane):
    shape = row.shape
    found = jnp.zeros(shape, F32)
    for r in range(table.shape[0]):
        line = jnp.broadcast_to(table[r : r + 1, :], shape)
        found = jnp.where(row == r, jnp.take_along_axis(line, lane, axis=1), found)
    return found


def dot_nt(left, right):
    return lax.dot_general(left, right, (((1,), (1,)), ((), ())), preferred_element_type=F32)


def render_kernel(
    params_hbm,
    cam_hbm,
    eye_hbm,
    tile_hbm,
    count_hbm,
    fetch_hbm,
    lists_hbm,
    target_hbm,
    rendered_ref,
    grads_ref,
    cams_ref,
    cam_ref,
    eye_ref,
    tile_ref,
    count_ref,
    fetch_ref,
    lists_ref,
    target_ref,
    pv,
    pj,
    ask,
    req,
    rowsend,
    rowsin,
    stage,
    stage_hi,
    lhs,
    rhs,
    alphas,
    weights,
    lanes,
    gsend,
    gin,
    turned,
    spare_ask,
    spare_rows,
    spare_grads,
    pos_ones,
    own_ones,
    in_sems,
    cam_sem,
    par_sem,
    send_sems,
    recv_sems,
):
    me = lax.axis_index("space")
    view = lax.axis_index("view")
    other = 1 - view

    def blank():
        stage[...] = jnp.zeros(stage.shape, F32)
        stage_hi[...] = jnp.zeros(stage.shape, F32)

    def lay(first, stride, value):
        stage[pl.ds(first, TILES, stride=stride), :] = value[:, 0:128]
        stage_hi[pl.ds(first, TILES, stride=stride), :] = value[:, 128:256]

    def take(first, stride):
        rows = pl.ds(first, TILES, stride=stride)
        return jnp.concatenate([stage[rows, :], stage_hi[rows, :]], axis=1)

    def staged(rows=slice(None)):
        return jnp.concatenate([stage[rows, :], stage_hi[rows, :]], axis=1)

    small = [
        pltpu.make_async_copy(src, dst, in_sems.at[i])
        for i, (src, dst) in enumerate(
            [
                (fetch_hbm, fetch_ref),
                (cam_hbm, cam_ref),
                (eye_hbm, eye_ref),
                (tile_hbm, tile_ref),
                (count_hbm, count_ref),
                (lists_hbm, lists_ref),
                (target_hbm, target_ref),
            ]
        )
    ]
    small[0].start()
    barrier = pltpu.get_barrier_semaphore()
    pl.semaphore_signal(barrier, inc=1, device_id=(me, other), device_id_type=MESH)

    def greet(d, c):
        pl.semaphore_signal(
            barrier, inc=1, device_id=(lax.rem(me + d, N), view), device_id_type=MESH
        )
        return c

    lax.fori_loop(1, N, greet, 0, unroll=7)
    loads = [
        pltpu.make_async_copy(
            params_hbm.at[:, pl.ds(128 * b, 128)], pv.at[pl.ds(PITCH * b, ROWS)], par_sem.at[b]
        )
        for b in range(COLS)
    ]
    for load in [*small[1:], *loads]:
        load.start()
    ask[...] = jnp.zeros(ask.shape, jnp.int32)
    rowsin[...] = jnp.zeros(rowsin.shape, F32)
    small[0].wait()
    ask[:, 0:CAP] = fetch_ref[...].T
    pl.semaphore_wait(barrier, N)

    def push(src, dst, device, sems):
        return pltpu.make_async_remote_copy(
            src_ref=src,
            dst_ref=dst,
            send_sem=send_sems.at[sems],
            recv_sem=recv_sems.at[sems],
            device_id=device,
            device_id_type=MESH,
        )

    def exchange(src, dst, own, sems):
        def one(d, c):
            t = lax.rem(me + d, N)
            push(
                src.at[pl.ds(t, 1)],
                dst.at[pl.ds(me if own else N + me, 1)],
                (t, view if own else other),
                sems,
            ).start()
            return c

        lax.fori_loop(1 if own else 0, N, one, 0, unroll=7 if own else 8)

    def finish_send(src, own, sems):
        push(src, src, (me, view), sems).wait_send()

    def finish_recv(dst, own, sems):
        rows = pl.ds(0, N) if own else pl.ds(N, N)
        push(dst.at[rows], dst.at[rows], (me, view), sems).wait_recv()

    def keep(src, dst, spare, sems):
        mine = src.at[pl.ds(me, 1)]
        pltpu.make_async_copy(mine, dst.at[pl.ds(me, 1)], recv_sems.at[sems]).start()
        pltpu.make_async_copy(mine, spare, send_sems.at[sems]).start()

    exchange(ask, req, True, 0)
    keep(ask, req, spare_ask, 0)
    for load in [*small[1:], *loads]:
        load.wait()
    camera = [[cam_ref[r, 0, c] for c in range(4)] for r in range(2)]
    eye = [eye_ref[0, c] for c in range(3)]
    values = [pv[pl.ds(p, COLS, stride=PITCH), :] for p in range(ROWS)]
    for f, row in enumerate(project(values, camera, eye)):
        pj[f] = row

    sheet = jnp.zeros((8, 128), F32)
    spots = [(r, c, camera[r][c]) for r in range(2) for c in range(4)]
    spots += [(3, c, eye[c]) for c in range(3)]
    for r, c, number in spots:
        here = (iota((8, 128), 0) == r) & (iota((8, 128), 1) == c)
        sheet = jnp.where(here, number, sheet)
    cams_ref[0:8, :] = sheet
    greeting = pltpu.make_async_remote_copy(
        src_ref=cams_ref.at[pl.ds(0, 8)],
        dst_ref=cams_ref.at[pl.ds(8, 8)],
        send_sem=cam_sem.at[0],
        recv_sem=cam_sem.at[1],
        device_id=(me, other),
        device_id_type=MESH,
    )
    greeting.start()

    finish_recv(req, True, 0)
    wanted = req[0:N, :].T[0:CAP, :]
    wanted = jnp.concatenate([wanted[0:8], wanted[8:16]], axis=1)
    want_row, want_lane = wanted >> 7, wanted & 127
    for f in range(FEATS):
        found = pick(pj[f], want_row, want_lane)
        stage[CAP * f : CAP * f + 8, :] = found
        stage[CAP * f + 8 : CAP * (f + 1), :] = pltpu.roll(found, N, 1)
    rowsend[...] = stage[...].T[0:N, :]
    exchange(rowsend, rowsin, True, 2)
    keep(rowsend, rowsin, spare_rows, 2)

    passed = pltpu.make_async_remote_copy(
        src_ref=req.at[pl.ds(0, N)],
        dst_ref=req.at[pl.ds(N, N)],
        send_sem=send_sems.at[1],
        recv_sem=recv_sems.at[1],
        device_id=(me, other),
        device_id_type=MESH,
    )
    passed.start()

    passed.wait_recv()
    turned[...] = req[...].T[0:CAP, :]

    def locate(j, found):
        line = turned[pl.ds(j, 1), :]
        line_hi, line_lo = line >> 7, line & 127
        hit = iota((COLS, 128), 0) == jnp.broadcast_to(line_hi, (COLS, 128))
        spot = iota((COLS, 128), 1).astype(F32)
        digits = jnp.concatenate(
            [
                jnp.where(hit, j.astype(F32), 0.0),
                jnp.where(hit, spot, 0.0),
            ],
            axis=0,
        ).astype(BF16)
        ones = jnp.where(
            iota((128, 128), 0) == jnp.broadcast_to(line_lo, (128, 128)), 1.0, 0.0
        ).astype(BF16)
        return found + dot_nt(digits, ones)

    found = lax.fori_loop(0, CAP, locate, jnp.zeros((2 * COLS, 128), F32))
    found_row = found[0:COLS].astype(jnp.int32)
    found_lane = found[COLS : 2 * COLS].astype(jnp.int32)
    own = found_lane < N

    pixel = iota((TILES, PX), 1)
    u = (pixel % 16).astype(F32) - 7.5
    w = (pixel // 16).astype(F32) - 7.5
    basis = [jnp.ones_like(u), u, w, u * u, u * w, w * w]
    blank()
    for c in range(6):
        for part in range(3):
            lay(3 * c + part, GROUP, basis[c])
    rhs[...] = staged().astype(BF16)

    for t in range(TILES):
        listed = lists_ref[t : t + 1, :]
        at_pos = iota((CAP, K), 0) == jnp.broadcast_to(listed & 15, (CAP, K))
        at_own = iota((N, K), 0) == jnp.broadcast_to(listed >> 4, (N, K))
        pos_ones[t] = jnp.where(at_pos, 1.0, 0.0).astype(BF16)
        own_ones[t] = jnp.where(at_own, 1.0, 0.0).astype(BF16)

    entry_row = lists_ref[...] & 7
    entry_lane = (lists_ref[...] >> 4) + ((lists_ref[...] & 8) << 3)
    finish_recv(rowsin, True, 2)
    stage[...] = rowsin[...].T

    entries = []
    for f in range(FEATS):
        first_half = stage[CAP * f : CAP * f + 8, :]
        second_half = stage[CAP * f + 8 : CAP * (f + 1), :]
        table = jnp.where(iota((8, 128), 1) < N, first_half, pltpu.roll(second_half, N, 1))
        entries.append(
            jnp.concatenate(
                [
                    pick(table, entry_row[:, h : h + 128], entry_lane[:, h : h + 128])
                    for h in (0, 128)
                ],
                axis=1,
            )
        )

    tile_row = iota((TILES, PX), 0)
    mid_x = jnp.zeros((TILES, PX), F32)
    mid_y = jnp.zeros((TILES, PX), F32)
    live = jnp.zeros((TILES, PX), jnp.int32)
    for t in range(TILES):
        here = tile_row == t
        mid_x = jnp.where(here, (tile_ref[0, t] % 32 * 16 + 8).astype(F32), mid_x)
        mid_y = jnp.where(here, (tile_ref[0, t] // 32 * 16 + 8).astype(F32), mid_y)
        live = jnp.where(here, count_ref[0, t], live)
    alive = pixel < live
    spot_x = entries[0] * 512.0 - mid_x
    spot_y = entries[1] * 512.0 - mid_y
    con_a, con_b, con_c = [entries[2 + i] * (1.0 / 262144.0) for i in range(3)]
    lin_x = con_a * spot_x + con_b * spot_y
    lin_y = con_c * spot_y + con_b * spot_x
    level = entries[5] - 0.5 * (spot_x * lin_x + spot_y * lin_y)
    coeffs = [level, lin_x, lin_y, -0.5 * con_a, -con_b, -0.5 * con_c]
    blank()
    for c in range(6):
        coeff = jnp.where(alive, coeffs[c] * LOG2E, -1e30 if c == 0 else 0.0)
        for part, piece in enumerate(split(coeff, 3)):
            lay(3 * c + part, GROUP, piece)
    colours = [jnp.where(alive, entries[6 + c], 0.0) for c in range(3)]
    for c in range(3):
        high, low, rest = split(colours[c], 3)
        for part, piece in enumerate((high, high, low)):
            lay(18 + 3 * c + part, GROUP, piece)
        lay(27 + c, GROUP, rest)
    lanes[...] = staged().T

    column = iota((TILES * GROUP, 128), 0) % GROUP
    wants = iota((TILES * GROUP, 128), 1)
    adds = (column == 18 + 3 * wants) | (column == 20 + 3 * wants) | (column == 27 + wants)
    chooser = jnp.where(adds & (wants < 3), 1.0, 0.0).astype(BF16)
    group_mask = iota((TILES, TILES * GROUP), 1) // GROUP == iota((TILES, TILES * GROUP), 0)

    def forward(step, carry):
        through, images = carry[0], list(carry[1:])
        first = pl.multiple_of(step * CHUNK, CHUNK)
        rows = pl.ds(pl.multiple_of(step * CHUNK * TILES, CHUNK * TILES), CHUNK * TILES)
        spread = jnp.where(
            group_mask[None], lanes[pl.ds(first, CHUNK), :][:, None, :], 0.0
        ).reshape(CHUNK * TILES, TILES * GROUP)
        low = spread.astype(BF16)
        lhs[rows, :] = low
        power = jnp.dot(low, rhs[...], preferred_element_type=F32)
        paint = jnp.dot(low, chooser, preferred_element_type=F32)
        alpha_all = jnp.exp2(power)
        alphas[rows, :] = alpha_all
        for i in range(CHUNK):
            alpha = alpha_all[i * TILES : (i + 1) * TILES]
            weight = through * alpha
            through = through * (1.0 - alpha)
            at = pl.ds(pl.multiple_of((first + i) * TILES, TILES), TILES)
            weights[at, :] = weight
            for c in range(3):
                shine = paint[i * TILES : (i + 1) * TILES, c : c + 1]
                images[c] = images[c] + weight * shine
        return (through, *images)

    zero = jnp.zeros((TILES, PX), F32)
    _, *images = lax.fori_loop(0, K // CHUNK, forward, (jnp.ones((TILES, PX), F32), zero, zero, zero), unroll=UNROLL_F)

    blank()
    shades = []
    for c in range(3):
        rendered_ref[c] = images[c]
        shade = (images[c] - target_ref[c]) * (1.0 / 256.0)
        high, low = split(shade, 2)
        shades.append(split(shade, 3))
        for part, piece in enumerate((high, low, high)):
            lay(18 + 3 * c + part, GROUP, piece)
    rhs[...] = staged().astype(BF16)
    blank()
    for c in range(6):
        lay(c, MOMS, basis[c])
    for c in range(3):
        for part in range(3):
            lay(128 + 6 + 3 * c + part, MOMS, shades[c][part])
    moment_rows = staged(slice(0, 128)).astype(BF16)
    shade_rows = staged(slice(128, 256)).astype(BF16)
    moment_mask = iota((TILES, 128), 1) // MOMS == iota((TILES, 128), 0)

    def backward(back, behind):
        step = K // CHUNK - 1 - back
        first = pl.multiple_of(step * CHUNK, CHUNK)
        rows = pl.ds(pl.multiple_of(step * CHUNK * TILES, CHUNK * TILES), CHUNK * TILES)
        tone = jnp.dot(lhs[rows, :], rhs[...], preferred_element_type=F32)
        alpha = alphas[rows, :]
        weight = weights[rows, :]
        slopes = [None] * CHUNK
        for i in reversed(range(CHUNK)):
            at = slice(i * TILES, (i + 1) * TILES)
            gap = tone[at] - behind
            slopes[i] = weight[at] * gap
            behind = behind * (1.0 - alpha[at]) + alpha[at] * tone[at]
        slope = jnp.concatenate(slopes, axis=0)
        total = jnp.zeros((CHUNK * TILES, 128), F32)
        for piece in split_low(slope, 2):
            total = total + dot_nt(piece, moment_rows)
        for piece in split_low(weight, 2):
            total = total + dot_nt(piece, shade_rows)
        total = jnp.where(moment_mask[None], total.reshape(CHUNK, TILES, 128), 0.0)
        lanes[pl.ds(first, CHUNK), 0:128] = jnp.sum(total, axis=1)
        return behind

    lax.fori_loop(0, K // CHUNK, backward, zero, unroll=UNROLL_B)

    turned_sums = lanes[:, 0:128].T
    stage[0:128, :] = turned_sums[:, 0:128]
    stage_hi[0:128, :] = turned_sums[:, 128:256]
    sums = [take(c, MOMS) for c in range(15)]
    s_1, s_u, s_w, s_uu, s_uw, s_ww = sums[0:6]
    d_x = s_u - spot_x * s_1
    d_y = s_w - spot_y * s_1
    d_xx = s_uu - 2.0 * spot_x * s_u + spot_x * spot_x * s_1
    d_yy = s_ww - 2.0 * spot_y * s_w + spot_y * spot_y * s_1
    d_xy = s_uw - spot_x * s_w - spot_y * s_u + spot_x * spot_y * s_1
    slopes = [
        512.0 * (con_a * d_x + con_b * d_y),
        512.0 * (con_c * d_y + con_b * d_x),
        d_xx * (-0.5 / 262144.0),
        d_xy * (-1.0 / 262144.0),
        d_yy * (-0.5 / 262144.0),
        s_1,
        *[sums[6 + 3 * c] + sums[7 + 3 * c] + sums[8 + 3 * c] for c in range(3)],
    ]
    blank()
    for f in range(FEATS):
        for part, piece in enumerate(split(jnp.where(alive, slopes[f], 0.0), 2)):
            lay(FEATS * part + f, GROUP, piece)

    total = jnp.zeros((2 * FEATS * CAP, N), F32)
    for t in range(TILES):
        block = staged(slice(t * GROUP, t * GROUP + 2 * FEATS)).astype(BF16)
        left = block[:, None, :] * pos_ones[t][None]
        total = total + dot_nt(left.reshape(2 * FEATS * CAP, K), own_ones[t])
    size = FEATS * CAP
    summed = total[0:size] + total[size : 2 * size]
    gsend[...] = jnp.zeros(gsend.shape, F32)
    gsend[:, 0:size] = summed.T

    exchange(gsend, gin, True, 3)
    keep(gsend, gin, spare_grads, 3)
    exchange(gsend, gin, False, 4)

    greeting.wait_recv()

    def chosen(row, col):
        return jnp.where(
            own,
            jnp.broadcast_to(cams_ref[row : row + 1, col : col + 1], own.shape),
            jnp.broadcast_to(cams_ref[8 + row : 9 + row, col : col + 1], own.shape),
        )

    camera = [[chosen(r, c) for c in range(4)] for r in range(2)]
    eye = [chosen(3, c) for c in range(3)]
    values = [pv[pl.ds(p, COLS, stride=PITCH), :] for p in range(ROWS)]
    _, pull = jax.vjp(lambda rows: project(rows, camera, eye), values)

    finish_recv(gin, True, 3)
    finish_recv(gin, False, 4)
    stage[...] = gin[...].T

    found = [
        pick(stage[CAP * f : CAP * (f + 1), :], found_row, found_lane) for f in range(FEATS)
    ]
    (grads,) = pull(found)
    for p in range(ROWS):
        grads_ref[pl.ds(p, COLS, stride=PITCH), :] = grads[p]
    finish_send(ask, True, 0)
    passed.wait_send()
    finish_send(rowsend, True, 2)
    finish_send(gsend, True, 3)
    finish_send(gsend, False, 4)
    greeting.wait_send()


def hand_on(image_ref, blocks_ref, image_hbm, grads_hbm, sems):
    copies = [
        pltpu.make_async_copy(
            blocks_ref.at[pl.ds(PITCH * b, ROWS)], grads_hbm.at[:, pl.ds(128 * b, 128)], sems.at[b]
        )
        for b in range(COLS)
    ]
    copies.append(pltpu.make_async_copy(image_ref, image_hbm, sems.at[COLS]))
    for copy in copies:
        copy.start()
    for copy in copies:
        copy.wait()


def on_device(params, camera, eye_point, tile_of, fetch, lists, counts, target):
    vmem = pl.BlockSpec(memory_space=pltpu.VMEM)
    hbm = pl.BlockSpec(memory_space=pltpu.HBM)
    image, blocks = pl.pallas_call(
        render_kernel,
        out_shape=(
            pltpu.VMEM((3, TILES, PX), F32),
            pltpu.VMEM((COLS * PITCH, 128), F32),
        ),
        in_specs=[hbm] * 8,
        out_specs=(vmem, vmem),
        scratch_shapes=[
            pltpu.VMEM((16, 128), F32),
            pltpu.SMEM((3, 1, 4), F32),
            pltpu.SMEM((1, 3), F32),
            pltpu.SMEM((1, TILES), jnp.int32),
            pltpu.SMEM((1, TILES), jnp.int32),
            pltpu.VMEM((CAP, N), jnp.int32),
            pltpu.VMEM((TILES, K), jnp.int32),
            pltpu.VMEM((3, TILES, PX), F32),
            pltpu.VMEM((COLS * PITCH, 128), F32),
            pltpu.VMEM((FEATS, COLS, 128), F32),
            pltpu.VMEM((N, 128), jnp.int32),
            pltpu.VMEM((2 * N, 128), jnp.int32),
            pltpu.VMEM((N, 256), F32),
            pltpu.VMEM((2 * N, 256), F32),
            pltpu.VMEM((256, 128), F32),
            pltpu.VMEM((256, 128), F32),
            pltpu.VMEM((K * TILES, 256), BF16),
            pltpu.VMEM((256, PX), BF16),
            pltpu.VMEM((K * TILES, PX), F32),
            pltpu.VMEM((K * TILES, PX), F32),
            pltpu.VMEM((K, 256), F32),
            pltpu.VMEM((N, 256), F32),
            pltpu.VMEM((2 * N, 256), F32),
            pltpu.VMEM((CAP, 128), jnp.int32),
            pltpu.VMEM((1, 128), jnp.int32),
            pltpu.VMEM((1, 256), F32),
            pltpu.VMEM((1, 256), F32),
            pltpu.VMEM((TILES, CAP, K), BF16),
            pltpu.VMEM((TILES, N, K), BF16),
            pltpu.SemaphoreType.DMA((7,)),
            pltpu.SemaphoreType.DMA((2,)),
            pltpu.SemaphoreType.DMA((COLS,)),
            pltpu.SemaphoreType.DMA((5,)),
            pltpu.SemaphoreType.DMA((5,)),
        ],
        compiler_params=pltpu.CompilerParams(
            collective_id=0, has_side_effects=True, vmem_limit_bytes=40 << 20
        ),
        name="render",
    )(
        *[
            pltpu.with_memory_space_constraint(arg, pltpu.HBM)
            for arg in (
                params,
                camera.transpose(1, 0, 2),
                eye_point,
                tile_of,
                counts,
                fetch[0, 0].T,
                lists[0],
                target[0].transpose(1, 0, 2),
            )
        ]
    )
    rendered, grads = pl.pallas_call(
        hand_on,
        out_shape=(
            jax.ShapeDtypeStruct(image.shape, F32),
            jax.ShapeDtypeStruct(params.shape, F32),
        ),
        in_specs=[pl.BlockSpec(memory_space=pl.ANY)] * 2,
        out_specs=(hbm, hbm),
        scratch_shapes=[pltpu.SemaphoreType.DMA((COLS + 1,))],
        compiler_params=pltpu.CompilerParams(vmem_limit_bytes=4 << 20),
        name="hand_on",
    )(*[pltpu.with_memory_space_constraint(x, pltpu.VMEM) for x in (image, blocks)])
    return (rendered.transpose(1, 0, 2)[None], grads)


def solution(mesh):
    placed = (
        P(None, "space"),
        P("view", None, None),
        P("view", None),
        P("view", "space"),
        P("view", "space", None, None),
        P("view", "space", None),
        P("view", "space"),
        P("view", "space", None, None),
    )
    return jax.shard_map(
        on_device,
        mesh=mesh,
        in_specs=placed,
        out_specs=(P("view", "space", None, None), P(None, "space")),
        check_vma=False,
    )
```

```python
import functools

import jax
import jax.numpy as jnp
from jax import lax
from jax.experimental import pallas as pl
from jax.experimental.pallas import tpu as pltpu
from jax.sharding import PartitionSpec as P

DILATE = 0.3 / 262144.0
HARM_ZERO = 0.28209479177387814
HARM_ONE = 0.4886025119029199
HARM_TWO = (
    1.0925484305920792,
    -1.0925484305920792,
    0.31539156525252005,
    -1.0925484305920792,
    0.5462742152960396,
)
HARM_THREE = (
    -0.5900435899266435,
    2.890611442640554,
    -0.4570457994644658,
    0.3731763325901154,
    -0.4570457994644658,
    1.445305721320277,
    -0.5900435899266435,
)
LOG2E = 1.4426950408889634
MESH = pl.DeviceIdType.MESH
F32 = jnp.float32
BF16 = jnp.bfloat16

N = 64
CAP = 16
TILES = 8
K = 256
PX = 256
ROWS = 59
PITCH = 64
COLS = 16
FEATS = 9
GROUP = 32
MOMS = 16
CHUNK = 32


def hops(offset):
    return sum(min(step, 4 - step) for step in offset)


OFFSETS = sorted(
    [(dz, dy, dx) for dz in range(4) for dy in range(4) for dx in range(4)],
    key=lambda offset: (-hops(offset), offset),
)


def harmonics(dir_x, dir_y, dir_z):
    sq_x, sq_y, sq_z = (dir_x * dir_x, dir_y * dir_y, dir_z * dir_z)
    return [
        HARM_ZERO * jnp.ones_like(dir_x),
        -HARM_ONE * dir_y,
        HARM_ONE * dir_z,
        -HARM_ONE * dir_x,
        HARM_TWO[0] * dir_x * dir_y,
        HARM_TWO[1] * dir_y * dir_z,
        HARM_TWO[2] * (2.0 * sq_z - sq_x - sq_y),
        HARM_TWO[3] * dir_x * dir_z,
        HARM_TWO[4] * (sq_x - sq_y),
        HARM_THREE[0] * dir_y * (3.0 * sq_x - sq_y),
        HARM_THREE[1] * dir_x * dir_y * dir_z,
        HARM_THREE[2] * dir_y * (4.0 * sq_z - sq_x - sq_y),
        HARM_THREE[3] * dir_z * (2.0 * sq_z - 3.0 * sq_x - 3.0 * sq_y),
        HARM_THREE[4] * dir_x * (4.0 * sq_z - sq_x - sq_y),
        HARM_THREE[5] * dir_z * (sq_x - sq_y),
        HARM_THREE[6] * dir_x * (sq_x - 3.0 * sq_y),
    ]


def project(rows, camera, eye):
    centre = rows[0:3]
    scales = [jnp.exp(row) for row in rows[3:6]]
    quat = rows[6:10]
    norm = lax.rsqrt(sum(q * q for q in quat))
    q_w, q_x, q_y, q_z = [q * norm for q in quat]
    rotation = [
        [
            1.0 - 2.0 * (q_y * q_y + q_z * q_z),
            2.0 * (q_x * q_y - q_w * q_z),
            2.0 * (q_x * q_z + q_w * q_y),
        ],
        [
            2.0 * (q_x * q_y + q_w * q_z),
            1.0 - 2.0 * (q_x * q_x + q_z * q_z),
            2.0 * (q_y * q_z - q_w * q_x),
        ],
        [
            2.0 * (q_x * q_z - q_w * q_y),
            2.0 * (q_y * q_z + q_w * q_x),
            1.0 - 2.0 * (q_x * q_x + q_y * q_y),
        ],
    ]
    jacob = [
        [
            (
                camera[row][0] * rotation[0][col]
                + camera[row][1] * rotation[1][col]
                + camera[row][2] * rotation[2][col]
            )
            * scales[col]
            for col in range(3)
        ]
        for row in range(2)
    ]
    cov_xx = sum(j * j for j in jacob[0]) + DILATE
    cov_xy = sum(j * i for j, i in zip(jacob[0], jacob[1]))
    cov_yy = sum(j * j for j in jacob[1]) + DILATE
    inv_det = 1.0 / (cov_xx * cov_yy - cov_xy * cov_xy)
    screen = [
        camera[row][0] * centre[0]
        + camera[row][1] * centre[1]
        + camera[row][2] * centre[2]
        + camera[row][3]
        for row in range(2)
    ]
    logit = rows[10]
    log_opacity = jnp.minimum(logit, 0.0) - jnp.log1p(jnp.exp(-jnp.abs(logit)))
    offset = [c - e for c, e in zip(centre, eye)]
    inverse = lax.rsqrt(sum(o * o for o in offset) + 1.0)
    basis = harmonics(*[o * inverse for o in offset])
    colours = [
        jnp.maximum(sum(b * rows[11 + 3 * l + c] for l, b in enumerate(basis)) + 0.5, 0.0)
        for c in range(3)
    ]
    return [
        *screen,
        cov_yy * inv_det,
        -cov_xy * inv_det,
        cov_xx * inv_det,
        log_opacity,
        *colours,
    ]


def split(value, parts):
    pieces = []
    for _ in range(parts - 1):
        piece = value.astype(BF16).astype(F32)
        pieces.append(piece)
        value = value - piece
    return [*pieces, value.astype(BF16).astype(F32)]


def split_low(value, parts):
    pieces = []
    for _ in range(parts - 1):
        piece = value.astype(BF16)
        pieces.append(piece)
        value = value - piece.astype(F32)
    return [*pieces, value.astype(BF16)]


def iota(shape, dim):
    return lax.broadcasted_iota(jnp.int32, shape, dim)


def pick(table, row, lane):
    shape = row.shape
    found = jnp.zeros(shape, F32)
    for r in range(table.shape[0]):
        line = jnp.broadcast_to(table[r : r + 1, :], shape)
        found = jnp.where(row == r, jnp.take_along_axis(line, lane, axis=1), found)
    return found


def dot_nt(left, right):
    return lax.dot_general(left, right, (((1,), (1,)), ((), ())), preferred_element_type=F32)


def render_kernel(
    params_hbm,
    cam_hbm,
    eye_hbm,
    tile_hbm,
    count_hbm,
    fetch_hbm,
    lists_hbm,
    target_hbm,
    rendered_ref,
    grads_ref,
    cams_ref,
    cam_ref,
    eye_ref,
    tile_ref,
    count_ref,
    fetch_ref,
    lists_ref,
    target_ref,
    pv,
    pj,
    ask,
    req,
    rowsend,
    rowsin,
    stage,
    stage_hi,
    lhs,
    rhs,
    alphas,
    weights,
    lanes,
    gsend,
    gin,
    turned,
    spare_ask,
    spare_rows,
    spare_grads,
    pos_ones,
    own_ones,
    totals,
    tones,
    paints,
    pieces,
    in_sems,
    cam_sem,
    par_sem,
    send_sems,
    recv_sems,
):
    me = lax.axis_index("space")
    view = lax.axis_index("view")
    other = 1 - view
    along = [(me // 16, 16), (me // 4 % 4, 4), (me % 4, 1)]
    shifted = [[(at + step) % 4 * pitch for step in range(4)] for at, pitch in along]

    def device(offset):
        return sum(shifted[axis][step] for axis, step in enumerate(offset))

    def blank():
        stage[...] = jnp.zeros(stage.shape, F32)
        stage_hi[...] = jnp.zeros(stage.shape, F32)

    def lay(first, stride, value):
        stage[pl.ds(first, TILES, stride=stride), :] = value[:, 0:128]
        stage_hi[pl.ds(first, TILES, stride=stride), :] = value[:, 128:256]

    def take(first, stride):
        rows = pl.ds(first, TILES, stride=stride)
        return jnp.concatenate([stage[rows, :], stage_hi[rows, :]], axis=1)

    def staged(rows=slice(None)):
        return jnp.concatenate([stage[rows, :], stage_hi[rows, :]], axis=1)

    small = [
        pltpu.make_async_copy(src, dst, in_sems.at[i])
        for i, (src, dst) in enumerate(
            [
                (fetch_hbm, fetch_ref),
                (cam_hbm, cam_ref),
                (eye_hbm, eye_ref),
                (tile_hbm, tile_ref),
                (count_hbm, count_ref),
                (lists_hbm, lists_ref),
                (target_hbm, target_ref),
            ]
        )
    ]
    small[0].start()
    barrier = pltpu.get_barrier_semaphore()
    pl.semaphore_signal(barrier, inc=1, device_id=(me, other), device_id_type=MESH)

    for offset in OFFSETS[: N - 1]:
        pl.semaphore_signal(
            barrier, inc=1, device_id=(device(offset), view), device_id_type=MESH
        )
    loads = [
        pltpu.make_async_copy(
            params_hbm.at[:, pl.ds(128 * b, 128)], pv.at[pl.ds(PITCH * b, ROWS)], par_sem.at[b]
        )
        for b in range(COLS)
    ]
    for load in [*small[1:], *loads]:
        load.start()
    ask[...] = jnp.zeros(ask.shape, jnp.int32)
    rowsin[...] = jnp.zeros(rowsin.shape, F32)
    small[0].wait()
    ask[:, 0:CAP] = fetch_ref[...].T
    pl.semaphore_wait(barrier, N)

    def push(src, dst, device, sems):
        return pltpu.make_async_remote_copy(
            src_ref=src,
            dst_ref=dst,
            send_sem=send_sems.at[sems],
            recv_sem=recv_sems.at[sems],
            device_id=device,
            device_id_type=MESH,
        )

    def exchange(src, dst, own, sems):
        for offset in OFFSETS[: N - 1] if own else OFFSETS:
            t = device(offset)
            push(
                src.at[pl.ds(t, 1)],
                dst.at[pl.ds(me if own else N + me, 1)],
                (t, view if own else other),
                sems,
            ).start()

    def finish_send(src, own, sems):
        push(src, src, (me, view), sems).wait_send()

    def finish_recv(dst, own, sems):
        rows = pl.ds(0, N) if own else pl.ds(N, N)
        push(dst.at[rows], dst.at[rows], (me, view), sems).wait_recv()

    def keep(src, dst, spare, sems):
        mine = src.at[pl.ds(me, 1)]
        pltpu.make_async_copy(mine, dst.at[pl.ds(me, 1)], recv_sems.at[sems]).start()
        pltpu.make_async_copy(mine, spare, send_sems.at[sems]).start()

    exchange(ask, req, True, 0)
    keep(ask, req, spare_ask, 0)
    for load in [*small[1:], *loads]:
        load.wait()
    camera = [[cam_ref[r, 0, c] for c in range(4)] for r in range(2)]
    eye = [eye_ref[0, c] for c in range(3)]
    values = [pv[pl.ds(p, COLS, stride=PITCH), :] for p in range(ROWS)]
    for f, row in enumerate(project(values, camera, eye)):
        pj[f] = row

    sheet = jnp.zeros((8, 128), F32)
    spots = [(r, c, camera[r][c]) for r in range(2) for c in range(4)]
    spots += [(3, c, eye[c]) for c in range(3)]
    for r, c, number in spots:
        here = (iota((8, 128), 0) == r) & (iota((8, 128), 1) == c)
        sheet = jnp.where(here, number, sheet)
    cams_ref[0:8, :] = sheet
    greeting = pltpu.make_async_remote_copy(
        src_ref=cams_ref.at[pl.ds(0, 8)],
        dst_ref=cams_ref.at[pl.ds(8, 8)],
        send_sem=cam_sem.at[0],
        recv_sem=cam_sem.at[1],
        device_id=(me, other),
        device_id_type=MESH,
    )
    greeting.start()

    finish_recv(req, True, 0)
    wanted = req[0:N, :].T[0:CAP, :]
    wanted = jnp.concatenate([wanted[0:8], wanted[8:16]], axis=1)
    want_row, want_lane = wanted >> 7, wanted & 127
    for f in range(FEATS):
        found = pick(pj[f], want_row, want_lane)
        stage[CAP * f : CAP * f + 8, :] = found
        stage[CAP * f + 8 : CAP * (f + 1), :] = pltpu.roll(found, N, 1)
    rowsend[...] = stage[...].T[0:N, :]
    exchange(rowsend, rowsin, True, 2)
    keep(rowsend, rowsin, spare_rows, 2)

    passed = pltpu.make_async_remote_copy(
        src_ref=req.at[pl.ds(0, N)],
        dst_ref=req.at[pl.ds(N, N)],
        send_sem=send_sems.at[1],
        recv_sem=recv_sems.at[1],
        device_id=(me, other),
        device_id_type=MESH,
    )
    passed.start()

    passed.wait_recv()
    turned[...] = req[...].T[0:CAP, :]

    def locate(j, found):
        line = turned[pl.ds(j, 1), :]
        line_hi, line_lo = line >> 7, line & 127
        hit = iota((COLS, 128), 0) == jnp.broadcast_to(line_hi, (COLS, 128))
        spot = iota((COLS, 128), 1).astype(F32)
        digits = jnp.concatenate(
            [
                jnp.where(hit, j.astype(F32), 0.0),
                jnp.where(hit, spot, 0.0),
            ],
            axis=0,
        ).astype(BF16)
        ones = jnp.where(
            iota((128, 128), 0) == jnp.broadcast_to(line_lo, (128, 128)), 1.0, 0.0
        ).astype(BF16)
        return found + dot_nt(digits, ones)

    found = lax.fori_loop(0, CAP, locate, jnp.zeros((2 * COLS, 128), F32))
    found_row = found[0:COLS].astype(jnp.int32)
    found_lane = found[COLS : 2 * COLS].astype(jnp.int32)
    own = found_lane < N

    pixel = iota((TILES, PX), 1)
    u = (pixel % 16).astype(F32) - 7.5
    w = (pixel // 16).astype(F32) - 7.5
    basis = [jnp.ones_like(u), u, w, u * u, u * w, w * w]
    blank()
    for c in range(6):
        for part in range(3):
            lay(3 * c + part, GROUP, basis[c])
    rhs[...] = staged().astype(BF16)

    for t in range(TILES):
        listed = lists_ref[t : t + 1, :]
        at_pos = iota((CAP, K), 0) == jnp.broadcast_to(listed & 15, (CAP, K))
        at_own = iota((N, K), 0) == jnp.broadcast_to(listed >> 4, (N, K))
        pos_ones[t] = jnp.where(at_pos, 1.0, 0.0).astype(BF16)
        own_ones[t] = jnp.where(at_own, 1.0, 0.0).astype(BF16)

    entry_row = lists_ref[...] & 7
    entry_lane = (lists_ref[...] >> 4) + ((lists_ref[...] & 8) << 3)
    finish_recv(rowsin, True, 2)
    stage[...] = rowsin[...].T

    entries = []
    for f in range(FEATS):
        first_half = stage[CAP * f : CAP * f + 8, :]
        second_half = stage[CAP * f + 8 : CAP * (f + 1), :]
        table = jnp.where(iota((8, 128), 1) < N, first_half, pltpu.roll(second_half, N, 1))
        entries.append(
            jnp.concatenate(
                [
                    pick(table, entry_row[:, h : h + 128], entry_lane[:, h : h + 128])
                    for h in (0, 128)
                ],
                axis=1,
            )
        )

    tile_row = iota((TILES, PX), 0)
    mid_x = jnp.zeros((TILES, PX), F32)
    mid_y = jnp.zeros((TILES, PX), F32)
    live = jnp.zeros((TILES, PX), jnp.int32)
    for t in range(TILES):
        here = tile_row == t
        mid_x = jnp.where(here, (tile_ref[0, t] % 32 * 16 + 8).astype(F32), mid_x)
        mid_y = jnp.where(here, (tile_ref[0, t] // 32 * 16 + 8).astype(F32), mid_y)
        live = jnp.where(here, count_ref[0, t], live)
    alive = pixel < live
    spot_x = entries[0] * 512.0 - mid_x
    spot_y = entries[1] * 512.0 - mid_y
    con_a, con_b, con_c = [entries[2 + i] * (1.0 / 262144.0) for i in range(3)]
    lin_x = con_a * spot_x + con_b * spot_y
    lin_y = con_c * spot_y + con_b * spot_x
    level = entries[5] - 0.5 * (spot_x * lin_x + spot_y * lin_y)
    coeffs = [level, lin_x, lin_y, -0.5 * con_a, -con_b, -0.5 * con_c]
    blank()
    for c in range(6):
        coeff = jnp.where(alive, coeffs[c] * LOG2E, -1e30 if c == 0 else 0.0)
        for part, piece in enumerate(split(coeff, 3)):
            lay(3 * c + part, GROUP, piece)
    colours = [jnp.where(alive, entries[6 + c], 0.0) for c in range(3)]
    for c in range(3):
        high, low, rest = split(colours[c], 3)
        for part, piece in enumerate((high, high, low)):
            lay(18 + 3 * c + part, GROUP, piece)
        lay(27 + c, GROUP, rest)
    lanes[...] = staged().T

    column = iota((TILES * GROUP, 128), 0) % GROUP
    wants = iota((TILES * GROUP, 128), 1)
    adds = (column == 18 + 3 * wants) | (column == 20 + 3 * wants) | (column == 27 + wants)
    chooser = jnp.where(adds & (wants < 3), 1.0, 0.0).astype(BF16)
    group_mask = iota((TILES, TILES * GROUP), 1) // GROUP == iota((TILES, TILES * GROUP), 0)

    def chunk_rows(chunk):
        return slice(chunk * CHUNK * TILES, (chunk + 1) * CHUNK * TILES)

    def operands(chunk):
        line = lanes[chunk * CHUNK : (chunk + 1) * CHUNK, :]
        spread = jnp.where(group_mask[None], line[:, None, :], 0.0)
        lhs[chunk_rows(chunk), :] = spread.reshape(CHUNK * TILES, TILES * GROUP).astype(BF16)

    def exponents(chunk):
        rows = chunk_rows(chunk)
        power = jnp.dot(lhs[rows, :], rhs[...], preferred_element_type=F32)
        alphas[rows, :] = jnp.exp2(power)
        paints[rows, :] = jnp.dot(lhs[rows, :], chooser, preferred_element_type=F32)

    through = jnp.ones((TILES, PX), F32)
    images = [jnp.zeros((TILES, PX), F32)] * 3
    chunks = K // CHUNK
    for stage_no in range(chunks + 2):
        if stage_no < chunks:
            operands(stage_no)
        if 1 <= stage_no <= chunks:
            exponents(stage_no - 1)
        if stage_no >= 2:
            first = (stage_no - 2) * CHUNK * TILES
            for i in range(0, CHUNK, 2):
                pair = []
                for j in (i, i + 1):
                    at = slice(first + j * TILES, first + (j + 1) * TILES)
                    alpha = alphas[at, :]
                    weight = through * alpha
                    through = through * (1.0 - alpha)
                    weights[at, :] = weight
                    pair.append(weight)
                    for c in range(3):
                        images[c] = images[c] + weight * paints[at, c : c + 1]
                at = slice(first + i * TILES, first + (i + 2) * TILES)
                high, low = split_low(jnp.concatenate(pair, axis=0), 2)
                pieces[at, 2 * PX : 3 * PX] = high
                pieces[at, 3 * PX : 4 * PX] = low

    blank()
    shades = []
    for c in range(3):
        rendered_ref[c] = images[c]
        shade = (images[c] - target_ref[c]) * (1.0 / 256.0)
        high, low = split(shade, 2)
        shades.append(split(shade, 3))
        for part, piece in enumerate((high, low, high)):
            lay(18 + 3 * c + part, GROUP, piece)
    rhs[...] = staged().astype(BF16)
    blank()
    for c in range(6):
        lay(c, MOMS, basis[c])
    for c in range(3):
        for part in range(3):
            lay(128 + 6 + 3 * c + part, MOMS, shades[c][part])
    moment_rows = staged(slice(0, 128)).astype(BF16)
    shade_rows = staged(slice(128, 256)).astype(BF16)
    both_rows = jnp.concatenate([moment_rows, moment_rows, shade_rows, shade_rows], axis=1)

    def tone_of(chunk):
        rows = chunk_rows(chunk)
        tones[rows, :] = jnp.dot(lhs[rows, :], rhs[...], preferred_element_type=F32)

    def reductions(chunk):
        rows = chunk_rows(chunk)
        totals[rows, :] = dot_nt(pieces[rows, :], both_rows)

    behind = jnp.zeros((TILES, PX), F32)
    for stage_no in range(chunks + 2):
        if stage_no < chunks:
            tone_of(chunks - 1 - stage_no)
        if stage_no >= 2:
            reductions(chunks + 1 - stage_no)
        if 1 <= stage_no <= chunks:
            first = (chunks - stage_no) * CHUNK * TILES
            for i in reversed(range(0, CHUNK, 2)):
                pair = [None, None]
                for j in (1, 0):
                    at = slice(first + (i + j) * TILES, first + (i + j + 1) * TILES)
                    tone, alpha = tones[at, :], alphas[at, :]
                    pair[j] = weights[at, :] * (tone - behind)
                    behind = behind * (1.0 - alpha) + alpha * tone
                at = slice(first + i * TILES, first + (i + 2) * TILES)
                high, low = split_low(jnp.concatenate(pair, axis=0), 2)
                pieces[at, 0:PX] = high
                pieces[at, PX : 2 * PX] = low

    group = iota((K, 128), 1) // MOMS
    sums = totals[pl.ds(0, K, stride=TILES), :]
    for t in range(1, TILES):
        sums = jnp.where(group == t, totals[pl.ds(t, K, stride=TILES), :], sums)
    turned_sums = sums.T
    stage[0:128, :] = turned_sums[:, 0:128]
    stage_hi[0:128, :] = turned_sums[:, 128:256]
    sums = [take(c, MOMS) for c in range(15)]
    s_1, s_u, s_w, s_uu, s_uw, s_ww = sums[0:6]
    d_x = s_u - spot_x * s_1
    d_y = s_w - spot_y * s_1
    d_xx = s_uu - 2.0 * spot_x * s_u + spot_x * spot_x * s_1
    d_yy = s_ww - 2.0 * spot_y * s_w + spot_y * spot_y * s_1
    d_xy = s_uw - spot_x * s_w - spot_y * s_u + spot_x * spot_y * s_1
    slopes = [
        512.0 * (con_a * d_x + con_b * d_y),
        512.0 * (con_c * d_y + con_b * d_x),
        d_xx * (-0.5 / 262144.0),
        d_xy * (-1.0 / 262144.0),
        d_yy * (-0.5 / 262144.0),
        s_1,
        *[sums[6 + 3 * c] + sums[7 + 3 * c] + sums[8 + 3 * c] for c in range(3)],
    ]
    blank()
    for f in range(FEATS):
        for part, piece in enumerate(split(jnp.where(alive, slopes[f], 0.0), 2)):
            lay(FEATS * part + f, GROUP, piece)

    total = jnp.zeros((2 * FEATS * CAP, N), F32)
    for t in range(TILES):
        block = staged(slice(t * GROUP, t * GROUP + 2 * FEATS)).astype(BF16)
        left = block[:, None, :] * pos_ones[t][None]
        total = total + dot_nt(left.reshape(2 * FEATS * CAP, K), own_ones[t])
    size = FEATS * CAP
    summed = total[0:size] + total[size : 2 * size]
    gsend[...] = jnp.zeros(gsend.shape, F32)
    gsend[:, 0:size] = summed.T

    exchange(gsend, gin, True, 3)
    keep(gsend, gin, spare_grads, 3)
    exchange(gsend, gin, False, 4)

    greeting.wait_recv()

    def chosen(row, col):
        return jnp.where(
            own,
            jnp.broadcast_to(cams_ref[row : row + 1, col : col + 1], own.shape),
            jnp.broadcast_to(cams_ref[8 + row : 9 + row, col : col + 1], own.shape),
        )

    camera = [[chosen(r, c) for c in range(4)] for r in range(2)]
    eye = [chosen(3, c) for c in range(3)]
    values = [pv[pl.ds(p, COLS, stride=PITCH), :] for p in range(ROWS)]
    _, pull = jax.vjp(lambda rows: project(rows, camera, eye), values)

    finish_recv(gin, True, 3)
    finish_recv(gin, False, 4)
    stage[...] = gin[...].T

    found = [
        pick(stage[CAP * f : CAP * (f + 1), :], found_row, found_lane) for f in range(FEATS)
    ]
    (grads,) = pull(found)
    for p in range(ROWS):
        grads_ref[pl.ds(p, COLS, stride=PITCH), :] = grads[p]
    finish_send(ask, True, 0)
    passed.wait_send()
    finish_send(rowsend, True, 2)
    finish_send(gsend, True, 3)
    finish_send(gsend, False, 4)
    greeting.wait_send()


def hand_on(image_ref, blocks_ref, image_hbm, grads_hbm, sems):
    copies = [
        pltpu.make_async_copy(
            blocks_ref.at[pl.ds(PITCH * b, ROWS)], grads_hbm.at[:, pl.ds(128 * b, 128)], sems.at[b]
        )
        for b in range(COLS)
    ]
    copies.append(pltpu.make_async_copy(image_ref, image_hbm, sems.at[COLS]))
    for copy in copies:
        copy.start()
    for copy in copies:
        copy.wait()


def on_device(params, camera, eye_point, tile_of, fetch, lists, counts, target):
    vmem = pl.BlockSpec(memory_space=pltpu.VMEM)
    hbm = pl.BlockSpec(memory_space=pltpu.HBM)
    image, blocks = pl.pallas_call(
        render_kernel,
        out_shape=(
            pltpu.VMEM((3, TILES, PX), F32),
            pltpu.VMEM((COLS * PITCH, 128), F32),
        ),
        in_specs=[hbm] * 8,
        out_specs=(vmem, vmem),
        scratch_shapes=[
            pltpu.VMEM((16, 128), F32),
            pltpu.SMEM((3, 1, 4), F32),
            pltpu.SMEM((1, 3), F32),
            pltpu.SMEM((1, TILES), jnp.int32),
            pltpu.SMEM((1, TILES), jnp.int32),
            pltpu.VMEM((CAP, N), jnp.int32),
            pltpu.VMEM((TILES, K), jnp.int32),
            pltpu.VMEM((3, TILES, PX), F32),
            pltpu.VMEM((COLS * PITCH, 128), F32),
            pltpu.VMEM((FEATS, COLS, 128), F32),
            pltpu.VMEM((N, 128), jnp.int32),
            pltpu.VMEM((2 * N, 128), jnp.int32),
            pltpu.VMEM((N, 256), F32),
            pltpu.VMEM((2 * N, 256), F32),
            pltpu.VMEM((256, 128), F32),
            pltpu.VMEM((256, 128), F32),
            pltpu.VMEM((K * TILES, 256), BF16),
            pltpu.VMEM((256, PX), BF16),
            pltpu.VMEM((K * TILES, PX), F32),
            pltpu.VMEM((K * TILES, PX), F32),
            pltpu.VMEM((K, 256), F32),
            pltpu.VMEM((N, 256), F32),
            pltpu.VMEM((2 * N, 256), F32),
            pltpu.VMEM((CAP, 128), jnp.int32),
            pltpu.VMEM((1, 128), jnp.int32),
            pltpu.VMEM((1, 256), F32),
            pltpu.VMEM((1, 256), F32),
            pltpu.VMEM((TILES, CAP, K), BF16),
            pltpu.VMEM((TILES, N, K), BF16),
            pltpu.VMEM((K * TILES, 128), F32),
            pltpu.VMEM((K * TILES, PX), F32),
            pltpu.VMEM((K * TILES, 128), F32),
            pltpu.VMEM((K * TILES, 4 * PX), BF16),
            pltpu.SemaphoreType.DMA((7,)),
            pltpu.SemaphoreType.DMA((2,)),
            pltpu.SemaphoreType.DMA((COLS,)),
            pltpu.SemaphoreType.DMA((5,)),
            pltpu.SemaphoreType.DMA((5,)),
        ],
        compiler_params=pltpu.CompilerParams(
            collective_id=0, has_side_effects=True, vmem_limit_bytes=40 << 20
        ),
        name="render",
    )(
        *[
            pltpu.with_memory_space_constraint(arg, pltpu.HBM)
            for arg in (
                params,
                camera.transpose(1, 0, 2),
                eye_point,
                tile_of,
                counts,
                fetch[0, 0].T,
                lists[0],
                target[0].transpose(1, 0, 2),
            )
        ]
    )
    rendered, grads = pl.pallas_call(
        hand_on,
        out_shape=(
            jax.ShapeDtypeStruct(image.shape, F32),
            jax.ShapeDtypeStruct(params.shape, F32),
        ),
        in_specs=[pl.BlockSpec(memory_space=pl.ANY)] * 2,
        out_specs=(hbm, hbm),
        scratch_shapes=[pltpu.SemaphoreType.DMA((COLS + 1,))],
        compiler_params=pltpu.CompilerParams(vmem_limit_bytes=4 << 20),
        name="hand_on",
    )(*[pltpu.with_memory_space_constraint(x, pltpu.VMEM) for x in (image, blocks)])
    return (rendered.transpose(1, 0, 2)[None], grads)


def solution(mesh):
    placed = (
        P(None, "space"),
        P("view", None, None),
        P("view", None),
        P("view", "space"),
        P("view", "space", None, None),
        P("view", "space", None),
        P("view", "space"),
        P("view", "space", None, None),
    )
    return jax.shard_map(
        on_device,
        mesh=mesh,
        in_specs=placed,
        out_specs=(P("view", "space", None, None), P(None, "space")),
        check_vma=False,
    )
```

```python
import functools

import jax
import jax.numpy as jnp
from jax import lax
from jax.experimental import pallas as pl
from jax.experimental.pallas import tpu as pltpu
from jax.sharding import PartitionSpec as P

DILATE = 0.3 / 262144.0
HARM_ZERO = 0.28209479177387814
HARM_ONE = 0.4886025119029199
HARM_TWO = (
    1.0925484305920792,
    -1.0925484305920792,
    0.31539156525252005,
    -1.0925484305920792,
    0.5462742152960396,
)
HARM_THREE = (
    -0.5900435899266435,
    2.890611442640554,
    -0.4570457994644658,
    0.3731763325901154,
    -0.4570457994644658,
    1.445305721320277,
    -0.5900435899266435,
)
LOG2E = 1.4426950408889634
MESH = pl.DeviceIdType.MESH
F32 = jnp.float32
BF16 = jnp.bfloat16

N = 64
CAP = 16
TILES = 8
K = 256
PX = 256
ROWS = 59
PITCH = 64
COLS = 16
FEATS = 9
GROUP = 32
MOMS = 16
CHUNK = 32


def hops(offset):
    return sum(min(step, 4 - step) for step in offset)


OFFSETS = sorted(
    [(dz, dy, dx) for dz in range(4) for dy in range(4) for dx in range(4)],
    key=lambda offset: (-hops(offset), offset),
)


def harmonics(dir_x, dir_y, dir_z):
    sq_x, sq_y, sq_z = (dir_x * dir_x, dir_y * dir_y, dir_z * dir_z)
    return [
        HARM_ZERO * jnp.ones_like(dir_x),
        -HARM_ONE * dir_y,
        HARM_ONE * dir_z,
        -HARM_ONE * dir_x,
        HARM_TWO[0] * dir_x * dir_y,
        HARM_TWO[1] * dir_y * dir_z,
        HARM_TWO[2] * (2.0 * sq_z - sq_x - sq_y),
        HARM_TWO[3] * dir_x * dir_z,
        HARM_TWO[4] * (sq_x - sq_y),
        HARM_THREE[0] * dir_y * (3.0 * sq_x - sq_y),
        HARM_THREE[1] * dir_x * dir_y * dir_z,
        HARM_THREE[2] * dir_y * (4.0 * sq_z - sq_x - sq_y),
        HARM_THREE[3] * dir_z * (2.0 * sq_z - 3.0 * sq_x - 3.0 * sq_y),
        HARM_THREE[4] * dir_x * (4.0 * sq_z - sq_x - sq_y),
        HARM_THREE[5] * dir_z * (sq_x - sq_y),
        HARM_THREE[6] * dir_x * (sq_x - 3.0 * sq_y),
    ]


def project(rows, camera, eye):
    centre = rows[0:3]
    scales = [jnp.exp(row) for row in rows[3:6]]
    quat = rows[6:10]
    norm = lax.rsqrt(sum(q * q for q in quat))
    q_w, q_x, q_y, q_z = [q * norm for q in quat]
    rotation = [
        [
            1.0 - 2.0 * (q_y * q_y + q_z * q_z),
            2.0 * (q_x * q_y - q_w * q_z),
            2.0 * (q_x * q_z + q_w * q_y),
        ],
        [
            2.0 * (q_x * q_y + q_w * q_z),
            1.0 - 2.0 * (q_x * q_x + q_z * q_z),
            2.0 * (q_y * q_z - q_w * q_x),
        ],
        [
            2.0 * (q_x * q_z - q_w * q_y),
            2.0 * (q_y * q_z + q_w * q_x),
            1.0 - 2.0 * (q_x * q_x + q_y * q_y),
        ],
    ]
    jacob = [
        [
            (
                camera[row][0] * rotation[0][col]
                + camera[row][1] * rotation[1][col]
                + camera[row][2] * rotation[2][col]
            )
            * scales[col]
            for col in range(3)
        ]
        for row in range(2)
    ]
    cov_xx = sum(j * j for j in jacob[0]) + DILATE
    cov_xy = sum(j * i for j, i in zip(jacob[0], jacob[1]))
    cov_yy = sum(j * j for j in jacob[1]) + DILATE
    inv_det = 1.0 / (cov_xx * cov_yy - cov_xy * cov_xy)
    screen = [
        camera[row][0] * centre[0]
        + camera[row][1] * centre[1]
        + camera[row][2] * centre[2]
        + camera[row][3]
        for row in range(2)
    ]
    logit = rows[10]
    log_opacity = jnp.minimum(logit, 0.0) - jnp.log1p(jnp.exp(-jnp.abs(logit)))
    offset = [c - e for c, e in zip(centre, eye)]
    inverse = lax.rsqrt(sum(o * o for o in offset) + 1.0)
    basis = harmonics(*[o * inverse for o in offset])
    colours = [
        jnp.maximum(sum(b * rows[11 + 3 * l + c] for l, b in enumerate(basis)) + 0.5, 0.0)
        for c in range(3)
    ]
    return [
        *screen,
        cov_yy * inv_det,
        -cov_xy * inv_det,
        cov_xx * inv_det,
        log_opacity,
        *colours,
    ]


def split(value, parts):
    pieces = []
    for _ in range(parts - 1):
        piece = value.astype(BF16).astype(F32)
        pieces.append(piece)
        value = value - piece
    return [*pieces, value.astype(BF16).astype(F32)]


def split_low(value, parts):
    pieces = []
    for _ in range(parts - 1):
        piece = value.astype(BF16)
        pieces.append(piece)
        value = value - piece.astype(F32)
    return [*pieces, value.astype(BF16)]


def iota(shape, dim):
    return lax.broadcasted_iota(jnp.int32, shape, dim)


def pick(table, row, lane):
    shape = row.shape
    found = jnp.zeros(shape, F32)
    for r in range(table.shape[0]):
        line = jnp.broadcast_to(table[r : r + 1, :], shape)
        found = jnp.where(row == r, jnp.take_along_axis(line, lane, axis=1), found)
    return found


def dot_nt(left, right):
    return lax.dot_general(left, right, (((1,), (1,)), ((), ())), preferred_element_type=F32)


def render_kernel(
    params_hbm,
    cam_hbm,
    eye_hbm,
    tile_hbm,
    count_hbm,
    fetch_hbm,
    lists_hbm,
    target_hbm,
    rendered_ref,
    grads_ref,
    cams_ref,
    cam_ref,
    eye_ref,
    tile_ref,
    count_ref,
    fetch_ref,
    lists_ref,
    target_ref,
    pv,
    pj,
    ask,
    req,
    rowsend,
    rowsin,
    stage,
    stage_hi,
    lhs,
    rhs,
    alphas,
    weights,
    lanes,
    gsend,
    gin,
    turned,
    spare_ask,
    spare_rows,
    spare_grads,
    pos_ones,
    own_ones,
    totals,
    coef_lo,
    coef_hi,
    tone_lo,
    tone_hi,
    shade_lo,
    shade_hi,
    both_rows,
    tones,
    paints,
    pieces,
    in_sems,
    cam_sem,
    par_sem,
    send_sems,
    recv_sems,
):
    me = lax.axis_index("space")
    view = lax.axis_index("view")
    other = 1 - view
    along = [(me // 16, 16), (me // 4 % 4, 4), (me % 4, 1)]
    shifted = [[(at + step) % 4 * pitch for step in range(4)] for at, pitch in along]

    def device(offset):
        return sum(shifted[axis][step] for axis, step in enumerate(offset))

    places = [(stage, stage_hi), (coef_lo, coef_hi), (tone_lo, tone_hi), (shade_lo, shade_hi)]

    def blank():
        stage[...] = jnp.zeros(stage.shape, F32)
        stage_hi[...] = jnp.zeros(stage.shape, F32)

    def lay(first, stride, value, where=0):
        low, high = places[where]
        low[pl.ds(first, TILES, stride=stride), :] = value[:, 0:128]
        high[pl.ds(first, TILES, stride=stride), :] = value[:, 128:256]

    def take(first, stride):
        rows = pl.ds(first, TILES, stride=stride)
        return jnp.concatenate([stage[rows, :], stage_hi[rows, :]], axis=1)

    def staged(rows=slice(None), where=0):
        return jnp.concatenate([part[rows, :] for part in places[where]], axis=1)

    small = [
        pltpu.make_async_copy(src, dst, in_sems.at[i])
        for i, (src, dst) in enumerate(
            [
                (fetch_hbm, fetch_ref),
                (cam_hbm, cam_ref),
                (eye_hbm, eye_ref),
                (tile_hbm, tile_ref),
                (count_hbm, count_ref),
                (lists_hbm, lists_ref),
                (target_hbm, target_ref),
            ]
        )
    ]
    small[0].start()
    barrier = pltpu.get_barrier_semaphore()
    pl.semaphore_signal(barrier, inc=1, device_id=(me, other), device_id_type=MESH)

    for offset in OFFSETS[: N - 1]:
        pl.semaphore_signal(
            barrier, inc=1, device_id=(device(offset), view), device_id_type=MESH
        )
    loads = [
        pltpu.make_async_copy(
            params_hbm.at[:, pl.ds(128 * b, 128)], pv.at[pl.ds(PITCH * b, ROWS)], par_sem.at[b]
        )
        for b in range(COLS)
    ]
    for load in [*small[1:], *loads]:
        load.start()
    ask[...] = jnp.zeros(ask.shape, jnp.int32)
    rowsin[...] = jnp.zeros(rowsin.shape, F32)
    small[0].wait()
    ask[:, 0:CAP] = fetch_ref[...].T
    pl.semaphore_wait(barrier, N)

    def push(src, dst, device, sems):
        return pltpu.make_async_remote_copy(
            src_ref=src,
            dst_ref=dst,
            send_sem=send_sems.at[sems],
            recv_sem=recv_sems.at[sems],
            device_id=device,
            device_id_type=MESH,
        )

    def exchange(src, dst, own, sems):
        for offset in OFFSETS[: N - 1] if own else OFFSETS:
            t = device(offset)
            push(
                src.at[pl.ds(t, 1)],
                dst.at[pl.ds(me if own else N + me, 1)],
                (t, view if own else other),
                sems,
            ).start()

    def finish_send(src, own, sems):
        push(src, src, (me, view), sems).wait_send()

    def finish_recv(dst, own, sems):
        rows = pl.ds(0, N) if own else pl.ds(N, N)
        push(dst.at[rows], dst.at[rows], (me, view), sems).wait_recv()

    def keep(src, dst, spare, sems):
        mine = src.at[pl.ds(me, 1)]
        pltpu.make_async_copy(mine, dst.at[pl.ds(me, 1)], recv_sems.at[sems]).start()
        pltpu.make_async_copy(mine, spare, send_sems.at[sems]).start()

    exchange(ask, req, True, 0)
    keep(ask, req, spare_ask, 0)
    for load in [*small[1:], *loads]:
        load.wait()
    camera = [[cam_ref[r, 0, c] for c in range(4)] for r in range(2)]
    eye = [eye_ref[0, c] for c in range(3)]
    values = [pv[pl.ds(p, COLS, stride=PITCH), :] for p in range(ROWS)]
    for f, row in enumerate(project(values, camera, eye)):
        pj[f] = row

    sheet = jnp.zeros((8, 128), F32)
    spots = [(r, c, camera[r][c]) for r in range(2) for c in range(4)]
    spots += [(3, c, eye[c]) for c in range(3)]
    for r, c, number in spots:
        here = (iota((8, 128), 0) == r) & (iota((8, 128), 1) == c)
        sheet = jnp.where(here, number, sheet)
    cams_ref[0:8, :] = sheet
    greeting = pltpu.make_async_remote_copy(
        src_ref=cams_ref.at[pl.ds(0, 8)],
        dst_ref=cams_ref.at[pl.ds(8, 8)],
        send_sem=cam_sem.at[0],
        recv_sem=cam_sem.at[1],
        device_id=(me, other),
        device_id_type=MESH,
    )
    greeting.start()

    finish_recv(req, True, 0)
    wanted = req[0:N, :].T[0:CAP, :]
    wanted = jnp.concatenate([wanted[0:8], wanted[8:16]], axis=1)
    want_row, want_lane = wanted >> 7, wanted & 127
    for f in range(FEATS):
        found = pick(pj[f], want_row, want_lane)
        stage[CAP * f : CAP * f + 8, :] = found
        stage[CAP * f + 8 : CAP * (f + 1), :] = pltpu.roll(found, N, 1)
    rowsend[...] = stage[...].T[0:N, :]
    exchange(rowsend, rowsin, True, 2)
    keep(rowsend, rowsin, spare_rows, 2)

    passed = pltpu.make_async_remote_copy(
        src_ref=req.at[pl.ds(0, N)],
        dst_ref=req.at[pl.ds(N, N)],
        send_sem=send_sems.at[1],
        recv_sem=recv_sems.at[1],
        device_id=(me, other),
        device_id_type=MESH,
    )
    passed.start()

    passed.wait_recv()
    turned[...] = req[...].T[0:CAP, :]

    def locate(j, found):
        line = turned[pl.ds(j, 1), :]
        line_hi, line_lo = line >> 7, line & 127
        hit = iota((COLS, 128), 0) == jnp.broadcast_to(line_hi, (COLS, 128))
        spot = iota((COLS, 128), 1).astype(F32)
        digits = jnp.concatenate(
            [
                jnp.where(hit, j.astype(F32), 0.0),
                jnp.where(hit, spot, 0.0),
            ],
            axis=0,
        ).astype(BF16)
        ones = jnp.where(
            iota((128, 128), 0) == jnp.broadcast_to(line_lo, (128, 128)), 1.0, 0.0
        ).astype(BF16)
        return found + dot_nt(digits, ones)

    found = lax.fori_loop(0, CAP, locate, jnp.zeros((2 * COLS, 128), F32))
    found_row = found[0:COLS].astype(jnp.int32)
    found_lane = found[COLS : 2 * COLS].astype(jnp.int32)
    own = found_lane < N

    pixel = iota((TILES, PX), 1)
    u = (pixel % 16).astype(F32) - 7.5
    w = (pixel // 16).astype(F32) - 7.5
    basis = [jnp.ones_like(u), u, w, u * u, u * w, w * w]
    blank()
    for c in range(6):
        for part in range(3):
            lay(3 * c + part, GROUP, basis[c])
    rhs[...] = staged().astype(BF16)
    blank()
    for c in range(6):
        lay(c, MOMS, basis[c])
    both_rows[:, 0:PX] = staged(slice(0, 128)).astype(BF16)
    both_rows[:, PX : 2 * PX] = staged(slice(0, 128)).astype(BF16)
    for pair in places[1:]:
        for part in pair:
            part[...] = jnp.zeros(part.shape, F32)
    gsend[...] = jnp.zeros(gsend.shape, F32)

    for t in range(TILES):
        listed = lists_ref[t : t + 1, :]
        at_pos = iota((CAP, K), 0) == jnp.broadcast_to(listed & 15, (CAP, K))
        at_own = iota((N, K), 0) == jnp.broadcast_to(listed >> 4, (N, K))
        pos_ones[t] = jnp.where(at_pos, 1.0, 0.0).astype(BF16)
        own_ones[t] = jnp.where(at_own, 1.0, 0.0).astype(BF16)

    entry_row = lists_ref[...] & 7
    entry_lane = (lists_ref[...] >> 4) + ((lists_ref[...] & 8) << 3)
    finish_recv(rowsin, True, 2)
    stage[...] = rowsin[...].T

    entries = []
    for f in range(FEATS):
        first_half = stage[CAP * f : CAP * f + 8, :]
        second_half = stage[CAP * f + 8 : CAP * (f + 1), :]
        table = jnp.where(iota((8, 128), 1) < N, first_half, pltpu.roll(second_half, N, 1))
        entries.append(
            jnp.concatenate(
                [
                    pick(table, entry_row[:, h : h + 128], entry_lane[:, h : h + 128])
                    for h in (0, 128)
                ],
                axis=1,
            )
        )

    tile_row = iota((TILES, PX), 0)
    mid_x = jnp.zeros((TILES, PX), F32)
    mid_y = jnp.zeros((TILES, PX), F32)
    live = jnp.zeros((TILES, PX), jnp.int32)
    for t in range(TILES):
        here = tile_row == t
        mid_x = jnp.where(here, (tile_ref[0, t] % 32 * 16 + 8).astype(F32), mid_x)
        mid_y = jnp.where(here, (tile_ref[0, t] // 32 * 16 + 8).astype(F32), mid_y)
        live = jnp.where(here, count_ref[0, t], live)
    alive = pixel < live
    spot_x = entries[0] * 512.0 - mid_x
    spot_y = entries[1] * 512.0 - mid_y
    con_a, con_b, con_c = [entries[2 + i] * (1.0 / 262144.0) for i in range(3)]
    lin_x = con_a * spot_x + con_b * spot_y
    lin_y = con_c * spot_y + con_b * spot_x
    level = entries[5] - 0.5 * (spot_x * lin_x + spot_y * lin_y)
    coeffs = [level, lin_x, lin_y, -0.5 * con_a, -con_b, -0.5 * con_c]
    for c in range(6):
        coeff = jnp.where(alive, coeffs[c] * LOG2E, -1e30 if c == 0 else 0.0)
        for part, piece in enumerate(split(coeff, 3)):
            lay(3 * c + part, GROUP, piece, 1)
    colours = [jnp.where(alive, entries[6 + c], 0.0) for c in range(3)]
    for c in range(3):
        high, low, rest = split(colours[c], 3)
        for part, piece in enumerate((high, high, low)):
            lay(18 + 3 * c + part, GROUP, piece, 1)
        lay(27 + c, GROUP, rest, 1)
    lanes[...] = staged(where=1).T

    column = iota((TILES * GROUP, 3 * 128), 0) % GROUP
    wants = iota((TILES * GROUP, 3 * 128), 1) // 128
    adds = (column == 18 + 3 * wants) | (column == 20 + 3 * wants) | (column == 27 + wants)
    chooser = jnp.where(adds, 1.0, 0.0).astype(BF16)
    group_mask = iota((TILES, TILES * GROUP), 1) // GROUP == iota((TILES, TILES * GROUP), 0)

    def chunk_rows(chunk):
        return slice(chunk * CHUNK * TILES, (chunk + 1) * CHUNK * TILES)

    def operands(chunk):
        line = lanes[chunk * CHUNK : (chunk + 1) * CHUNK, :]
        spread = jnp.where(group_mask[None], line[:, None, :], 0.0)
        lhs[chunk_rows(chunk), :] = spread.reshape(CHUNK * TILES, TILES * GROUP).astype(BF16)

    def exponents(chunk):
        rows = chunk_rows(chunk)
        power = jnp.dot(lhs[rows, :], rhs[...], preferred_element_type=F32)
        alphas[rows, :] = jnp.exp2(power)
        paints[rows, :] = jnp.dot(lhs[rows, :], chooser, preferred_element_type=F32)

    through = jnp.ones((TILES, PX), F32)
    images = [jnp.zeros((TILES, PX), F32)] * 3
    chunks = K // CHUNK
    for stage_no in range(chunks + 2):
        if stage_no < chunks:
            operands(stage_no)
        if 1 <= stage_no <= chunks:
            exponents(stage_no - 1)
        if stage_no >= 2:
            first = (stage_no - 2) * CHUNK * TILES
            for i in range(0, CHUNK, 2):
                pair = []
                for j in (i, i + 1):
                    at = slice(first + j * TILES, first + (j + 1) * TILES)
                    alpha = alphas[at, :]
                    weight = through * alpha
                    through = through * (1.0 - alpha)
                    weights[at, :] = weight
                    pair.append(weight)
                    for c in range(3):
                        paint = paints[at, 128 * c : 128 * c + 128]
                        images[c] = images[c] + weight * jnp.concatenate([paint, paint], axis=1)
                at = slice(first + i * TILES, first + (i + 2) * TILES)
                high, low = split_low(jnp.concatenate(pair, axis=0), 2)
                pieces[at, 2 * PX : 3 * PX] = high
                pieces[at, 3 * PX : 4 * PX] = low

    for c in range(3):
        rendered_ref[c] = images[c]
        shade = (images[c] - target_ref[c]) * (1.0 / 256.0)
        high, low = split(shade, 2)
        for part, piece in enumerate((high, low, high)):
            lay(18 + 3 * c + part, GROUP, piece, 2)
        for part, piece in enumerate(split(shade, 3)):
            lay(6 + 3 * c + part, MOMS, piece, 3)
    rhs[...] = staged(where=2).astype(BF16)
    both_rows[:, 2 * PX : 3 * PX] = staged(where=3).astype(BF16)
    both_rows[:, 3 * PX : 4 * PX] = staged(where=3).astype(BF16)

    def tone_of(chunk):
        rows = chunk_rows(chunk)
        tones[rows, :] = jnp.dot(lhs[rows, :], rhs[...], preferred_element_type=F32)

    def reductions(chunk):
        rows = chunk_rows(chunk)
        totals[rows, :] = dot_nt(pieces[rows, :], both_rows[...])

    behind = jnp.zeros((TILES, PX), F32)
    for stage_no in range(chunks + 2):
        if stage_no < chunks:
            tone_of(chunks - 1 - stage_no)
        if stage_no >= 2:
            reductions(chunks + 1 - stage_no)
        if 1 <= stage_no <= chunks:
            first = (chunks - stage_no) * CHUNK * TILES
            for i in reversed(range(0, CHUNK, 2)):
                pair = [None, None]
                for j in (1, 0):
                    at = slice(first + (i + j) * TILES, first + (i + j + 1) * TILES)
                    tone, alpha = tones[at, :], alphas[at, :]
                    pair[j] = weights[at, :] * (tone - behind)
                    behind = behind * (1.0 - alpha) + alpha * tone
                at = slice(first + i * TILES, first + (i + 2) * TILES)
                high, low = split_low(jnp.concatenate(pair, axis=0), 2)
                pieces[at, 0:PX] = high
                pieces[at, PX : 2 * PX] = low

    group = iota((K, 128), 1) // MOMS
    sums = totals[pl.ds(0, K, stride=TILES), :]
    for t in range(1, TILES):
        sums = jnp.where(group == t, totals[pl.ds(t, K, stride=TILES), :], sums)
    turned_sums = sums.T
    stage[0:128, :] = turned_sums[:, 0:128]
    stage_hi[0:128, :] = turned_sums[:, 128:256]
    sums = [take(c, MOMS) for c in range(15)]
    s_1, s_u, s_w, s_uu, s_uw, s_ww = sums[0:6]
    d_x = s_u - spot_x * s_1
    d_y = s_w - spot_y * s_1
    d_xx = s_uu - 2.0 * spot_x * s_u + spot_x * spot_x * s_1
    d_yy = s_ww - 2.0 * spot_y * s_w + spot_y * spot_y * s_1
    d_xy = s_uw - spot_x * s_w - spot_y * s_u + spot_x * spot_y * s_1
    slopes = [
        512.0 * (con_a * d_x + con_b * d_y),
        512.0 * (con_c * d_y + con_b * d_x),
        d_xx * (-0.5 / 262144.0),
        d_xy * (-1.0 / 262144.0),
        d_yy * (-0.5 / 262144.0),
        s_1,
        *[sums[6 + 3 * c] + sums[7 + 3 * c] + sums[8 + 3 * c] for c in range(3)],
    ]
    for f in range(FEATS):
        for part, piece in enumerate(split(jnp.where(alive, slopes[f], 0.0), 2)):
            lay(FEATS * part + f, GROUP, piece)

    total = jnp.zeros((2 * FEATS * CAP, N), F32)
    for t in range(TILES):
        block = staged(slice(t * GROUP, t * GROUP + 2 * FEATS)).astype(BF16)
        left = block[:, None, :] * pos_ones[t][None]
        total = total + dot_nt(left.reshape(2 * FEATS * CAP, K), own_ones[t])
    size = FEATS * CAP
    summed = total[0:size] + total[size : 2 * size]
    gsend[:, 0:size] = summed.T

    for offset in OFFSETS:
        t = device(offset)
        for own_view in (True, False):
            if any(offset) or not own_view:
                push(
                    gsend.at[pl.ds(t, 1)],
                    gin.at[pl.ds(me if own_view else N + me, 1)],
                    (t, view if own_view else other),
                    3 if own_view else 4,
                ).start()
    keep(gsend, gin, spare_grads, 3)

    greeting.wait_recv()

    def chosen(row, col):
        return jnp.where(
            own,
            jnp.broadcast_to(cams_ref[row : row + 1, col : col + 1], own.shape),
            jnp.broadcast_to(cams_ref[8 + row : 9 + row, col : col + 1], own.shape),
        )

    camera = [[chosen(r, c) for c in range(4)] for r in range(2)]
    eye = [chosen(3, c) for c in range(3)]
    values = [pv[pl.ds(p, COLS, stride=PITCH), :] for p in range(ROWS)]
    _, pull = jax.vjp(lambda rows: project(rows, camera, eye), values)

    finish_recv(gin, True, 3)
    finish_recv(gin, False, 4)
    stage[...] = gin[...].T

    found = [
        pick(stage[CAP * f : CAP * (f + 1), :], found_row, found_lane) for f in range(FEATS)
    ]
    (grads,) = pull(found)
    for p in range(ROWS):
        grads_ref[pl.ds(p, COLS, stride=PITCH), :] = grads[p]
    finish_send(ask, True, 0)
    passed.wait_send()
    finish_send(rowsend, True, 2)
    finish_send(gsend, True, 3)
    finish_send(gsend, False, 4)
    greeting.wait_send()


def hand_on(image_ref, blocks_ref, image_hbm, grads_hbm, sems):
    copies = [
        pltpu.make_async_copy(
            blocks_ref.at[pl.ds(PITCH * b, ROWS)], grads_hbm.at[:, pl.ds(128 * b, 128)], sems.at[b]
        )
        for b in range(COLS)
    ]
    copies.append(pltpu.make_async_copy(image_ref, image_hbm, sems.at[COLS]))
    for copy in copies:
        copy.start()
    for copy in copies:
        copy.wait()


def on_device(params, camera, eye_point, tile_of, fetch, lists, counts, target):
    vmem = pl.BlockSpec(memory_space=pltpu.VMEM)
    hbm = pl.BlockSpec(memory_space=pltpu.HBM)
    image, blocks = pl.pallas_call(
        render_kernel,
        out_shape=(
            pltpu.VMEM((3, TILES, PX), F32),
            pltpu.VMEM((COLS * PITCH, 128), F32),
        ),
        in_specs=[hbm] * 8,
        out_specs=(vmem, vmem),
        scratch_shapes=[
            pltpu.VMEM((16, 128), F32),
            pltpu.SMEM((3, 1, 4), F32),
            pltpu.SMEM((1, 3), F32),
            pltpu.SMEM((1, TILES), jnp.int32),
            pltpu.SMEM((1, TILES), jnp.int32),
            pltpu.VMEM((CAP, N), jnp.int32),
            pltpu.VMEM((TILES, K), jnp.int32),
            pltpu.VMEM((3, TILES, PX), F32),
            pltpu.VMEM((COLS * PITCH, 128), F32),
            pltpu.VMEM((FEATS, COLS, 128), F32),
            pltpu.VMEM((N, 128), jnp.int32),
            pltpu.VMEM((2 * N, 128), jnp.int32),
            pltpu.VMEM((N, 256), F32),
            pltpu.VMEM((2 * N, 256), F32),
            pltpu.VMEM((256, 128), F32),
            pltpu.VMEM((256, 128), F32),
            pltpu.VMEM((K * TILES, 256), BF16),
            pltpu.VMEM((256, PX), BF16),
            pltpu.VMEM((K * TILES, PX), F32),
            pltpu.VMEM((K * TILES, PX), F32),
            pltpu.VMEM((K, 256), F32),
            pltpu.VMEM((N, 256), F32),
            pltpu.VMEM((2 * N, 256), F32),
            pltpu.VMEM((CAP, 128), jnp.int32),
            pltpu.VMEM((1, 128), jnp.int32),
            pltpu.VMEM((1, 256), F32),
            pltpu.VMEM((1, 256), F32),
            pltpu.VMEM((TILES, CAP, K), BF16),
            pltpu.VMEM((TILES, N, K), BF16),
            pltpu.VMEM((K * TILES, 128), F32),
            pltpu.VMEM((TILES * GROUP, 128), F32),
            pltpu.VMEM((TILES * GROUP, 128), F32),
            pltpu.VMEM((TILES * GROUP, 128), F32),
            pltpu.VMEM((TILES * GROUP, 128), F32),
            pltpu.VMEM((TILES * MOMS, 128), F32),
            pltpu.VMEM((TILES * MOMS, 128), F32),
            pltpu.VMEM((TILES * MOMS, 4 * PX), BF16),
            pltpu.VMEM((K * TILES, PX), F32),
            pltpu.VMEM((K * TILES, 3 * 128), F32),
            pltpu.VMEM((K * TILES, 4 * PX), BF16),
            pltpu.SemaphoreType.DMA((7,)),
            pltpu.SemaphoreType.DMA((2,)),
            pltpu.SemaphoreType.DMA((COLS,)),
            pltpu.SemaphoreType.DMA((5,)),
            pltpu.SemaphoreType.DMA((5,)),
        ],
        compiler_params=pltpu.CompilerParams(
            collective_id=0, has_side_effects=True, vmem_limit_bytes=40 << 20
        ),
        name="render",
    )(
        *[
            pltpu.with_memory_space_constraint(arg, pltpu.HBM)
            for arg in (
                params,
                camera.transpose(1, 0, 2),
                eye_point,
                tile_of,
                counts,
                fetch[0, 0].T,
                lists[0],
                target[0].transpose(1, 0, 2),
            )
        ]
    )
    rendered, grads = pl.pallas_call(
        hand_on,
        out_shape=(
            jax.ShapeDtypeStruct(image.shape, F32),
            jax.ShapeDtypeStruct(params.shape, F32),
        ),
        in_specs=[pl.BlockSpec(memory_space=pl.ANY)] * 2,
        out_specs=(hbm, hbm),
        scratch_shapes=[pltpu.SemaphoreType.DMA((COLS + 1,))],
        compiler_params=pltpu.CompilerParams(vmem_limit_bytes=4 << 20),
        name="hand_on",
    )(*[pltpu.with_memory_space_constraint(x, pltpu.VMEM) for x in (image, blocks)])
    return (rendered.transpose(1, 0, 2)[None], grads)


def solution(mesh):
    placed = (
        P(None, "space"),
        P("view", None, None),
        P("view", None),
        P("view", "space"),
        P("view", "space", None, None),
        P("view", "space", None),
        P("view", "space"),
        P("view", "space", None, None),
    )
    return jax.shard_map(
        on_device,
        mesh=mesh,
        in_specs=placed,
        out_specs=(P("view", "space", None, None), P(None, "space")),
        check_vma=False,
    )
```

```python
import functools

import jax
import jax.numpy as jnp
from jax import lax
from jax.experimental import pallas as pl
from jax.experimental.pallas import tpu as pltpu
from jax.sharding import PartitionSpec as P

DILATE = 0.3 / 262144.0
HARM_ZERO = 0.28209479177387814
HARM_ONE = 0.4886025119029199
HARM_TWO = (
    1.0925484305920792,
    -1.0925484305920792,
    0.31539156525252005,
    -1.0925484305920792,
    0.5462742152960396,
)
HARM_THREE = (
    -0.5900435899266435,
    2.890611442640554,
    -0.4570457994644658,
    0.3731763325901154,
    -0.4570457994644658,
    1.445305721320277,
    -0.5900435899266435,
)
LOG2E = 1.4426950408889634
MESH = pl.DeviceIdType.MESH
F32 = jnp.float32
BF16 = jnp.bfloat16

N = 64
CAP = 16
TILES = 8
K = 256
PX = 256
ROWS = 59
PITCH = 64
COLS = 16
FEATS = 9
GROUP = 32
MOMS = 16
CHUNK = 32


def hops(offset):
    return sum(min(step, 4 - step) for step in offset)


OFFSETS = sorted(
    [(dz, dy, dx) for dz in range(4) for dy in range(4) for dx in range(4)],
    key=lambda offset: (-hops(offset), offset),
)


def harmonics(dir_x, dir_y, dir_z):
    sq_x, sq_y, sq_z = (dir_x * dir_x, dir_y * dir_y, dir_z * dir_z)
    return [
        HARM_ZERO * jnp.ones_like(dir_x),
        -HARM_ONE * dir_y,
        HARM_ONE * dir_z,
        -HARM_ONE * dir_x,
        HARM_TWO[0] * dir_x * dir_y,
        HARM_TWO[1] * dir_y * dir_z,
        HARM_TWO[2] * (2.0 * sq_z - sq_x - sq_y),
        HARM_TWO[3] * dir_x * dir_z,
        HARM_TWO[4] * (sq_x - sq_y),
        HARM_THREE[0] * dir_y * (3.0 * sq_x - sq_y),
        HARM_THREE[1] * dir_x * dir_y * dir_z,
        HARM_THREE[2] * dir_y * (4.0 * sq_z - sq_x - sq_y),
        HARM_THREE[3] * dir_z * (2.0 * sq_z - 3.0 * sq_x - 3.0 * sq_y),
        HARM_THREE[4] * dir_x * (4.0 * sq_z - sq_x - sq_y),
        HARM_THREE[5] * dir_z * (sq_x - sq_y),
        HARM_THREE[6] * dir_x * (sq_x - 3.0 * sq_y),
    ]


def project(rows, camera, eye):
    centre = rows[0:3]
    scales = [jnp.exp(row) for row in rows[3:6]]
    quat = rows[6:10]
    norm = lax.rsqrt(sum(q * q for q in quat))
    q_w, q_x, q_y, q_z = [q * norm for q in quat]
    rotation = [
        [
            1.0 - 2.0 * (q_y * q_y + q_z * q_z),
            2.0 * (q_x * q_y - q_w * q_z),
            2.0 * (q_x * q_z + q_w * q_y),
        ],
        [
            2.0 * (q_x * q_y + q_w * q_z),
            1.0 - 2.0 * (q_x * q_x + q_z * q_z),
            2.0 * (q_y * q_z - q_w * q_x),
        ],
        [
            2.0 * (q_x * q_z - q_w * q_y),
            2.0 * (q_y * q_z + q_w * q_x),
            1.0 - 2.0 * (q_x * q_x + q_y * q_y),
        ],
    ]
    jacob = [
        [
            (
                camera[row][0] * rotation[0][col]
                + camera[row][1] * rotation[1][col]
                + camera[row][2] * rotation[2][col]
            )
            * scales[col]
            for col in range(3)
        ]
        for row in range(2)
    ]
    cov_xx = sum(j * j for j in jacob[0]) + DILATE
    cov_xy = sum(j * i for j, i in zip(jacob[0], jacob[1]))
    cov_yy = sum(j * j for j in jacob[1]) + DILATE
    inv_det = 1.0 / (cov_xx * cov_yy - cov_xy * cov_xy)
    screen = [
        camera[row][0] * centre[0]
        + camera[row][1] * centre[1]
        + camera[row][2] * centre[2]
        + camera[row][3]
        for row in range(2)
    ]
    logit = rows[10]
    log_opacity = jnp.minimum(logit, 0.0) - jnp.log1p(jnp.exp(-jnp.abs(logit)))
    offset = [c - e for c, e in zip(centre, eye)]
    inverse = lax.rsqrt(sum(o * o for o in offset) + 1.0)
    basis = harmonics(*[o * inverse for o in offset])
    colours = [
        jnp.maximum(sum(b * rows[11 + 3 * l + c] for l, b in enumerate(basis)) + 0.5, 0.0)
        for c in range(3)
    ]
    return [
        *screen,
        cov_yy * inv_det,
        -cov_xy * inv_det,
        cov_xx * inv_det,
        log_opacity,
        *colours,
    ]


def split(value, parts):
    pieces = []
    for _ in range(parts - 1):
        piece = value.astype(BF16).astype(F32)
        pieces.append(piece)
        value = value - piece
    return [*pieces, value.astype(BF16).astype(F32)]


def split_low(value, parts):
    pieces = []
    for _ in range(parts - 1):
        piece = value.astype(BF16)
        pieces.append(piece)
        value = value - piece.astype(F32)
    return [*pieces, value.astype(BF16)]


def iota(shape, dim):
    return lax.broadcasted_iota(jnp.int32, shape, dim)


def pick(table, row, lane):
    shape = row.shape
    found = jnp.zeros(shape, F32)
    for r in range(table.shape[0]):
        line = jnp.broadcast_to(table[r : r + 1, :], shape)
        found = jnp.where(row == r, jnp.take_along_axis(line, lane, axis=1), found)
    return found


def dot_nt(left, right):
    return lax.dot_general(left, right, (((1,), (1,)), ((), ())), preferred_element_type=F32)


def render_kernel(
    params_hbm,
    cam_hbm,
    eye_hbm,
    tile_hbm,
    count_hbm,
    fetch_hbm,
    lists_hbm,
    target_hbm,
    rendered_ref,
    grads_ref,
    cams_ref,
    cam_ref,
    eye_ref,
    tile_ref,
    count_ref,
    fetch_ref,
    lists_ref,
    target_ref,
    pv,
    pj,
    ask,
    req,
    rowsend,
    rowsin,
    stage,
    stage_hi,
    lhs,
    rhs,
    alphas,
    weights,
    lanes,
    gsend,
    gin,
    turned,
    spare_ask,
    spare_rows,
    spare_grads,
    pos_ones,
    own_ones,
    totals,
    coef_lo,
    coef_hi,
    tone_lo,
    tone_hi,
    shade_lo,
    shade_hi,
    both_rows,
    tones,
    paints,
    pieces,
    in_sems,
    cam_sem,
    par_sem,
    send_sems,
    recv_sems,
):
    me = lax.axis_index("space")
    view = lax.axis_index("view")
    other = 1 - view
    along = [(me // 16, 16), (me // 4 % 4, 4), (me % 4, 1)]
    shifted = [[(at + step) % 4 * pitch for step in range(4)] for at, pitch in along]

    def device(offset):
        return sum(shifted[axis][step] for axis, step in enumerate(offset))

    places = [(stage, stage_hi), (coef_lo, coef_hi), (tone_lo, tone_hi), (shade_lo, shade_hi)]

    def blank():
        stage[...] = jnp.zeros(stage.shape, F32)
        stage_hi[...] = jnp.zeros(stage.shape, F32)

    def lay(first, stride, value, where=0):
        low, high = places[where]
        low[pl.ds(first, TILES, stride=stride), :] = value[:, 0:128]
        high[pl.ds(first, TILES, stride=stride), :] = value[:, 128:256]

    def take(first, stride):
        rows = pl.ds(first, TILES, stride=stride)
        return jnp.concatenate([stage[rows, :], stage_hi[rows, :]], axis=1)

    def staged(rows=slice(None), where=0):
        return jnp.concatenate([part[rows, :] for part in places[where]], axis=1)

    small = [
        pltpu.make_async_copy(src, dst, in_sems.at[i])
        for i, (src, dst) in enumerate(
            [
                (fetch_hbm, fetch_ref),
                (cam_hbm, cam_ref),
                (eye_hbm, eye_ref),
                (tile_hbm, tile_ref),
                (count_hbm, count_ref),
                (lists_hbm, lists_ref),
                (target_hbm, target_ref),
            ]
        )
    ]
    small[0].start()
    barrier = pltpu.get_barrier_semaphore()
    pl.semaphore_signal(barrier, inc=1, device_id=(me, other), device_id_type=MESH)

    for offset in OFFSETS[: N - 1]:
        pl.semaphore_signal(
            barrier, inc=1, device_id=(device(offset), view), device_id_type=MESH
        )
    loads = [
        pltpu.make_async_copy(
            params_hbm.at[:, pl.ds(128 * b, 128)], pv.at[pl.ds(PITCH * b, ROWS)], par_sem.at[b]
        )
        for b in range(COLS)
    ]
    for load in [*small[1:], *loads]:
        load.start()
    ask[...] = jnp.zeros(ask.shape, jnp.int32)
    rowsin[...] = jnp.zeros(rowsin.shape, F32)
    small[0].wait()
    ask[:, 0:CAP] = fetch_ref[...].T
    pl.semaphore_wait(barrier, N)

    def push(src, dst, device, sems):
        return pltpu.make_async_remote_copy(
            src_ref=src,
            dst_ref=dst,
            send_sem=send_sems.at[sems],
            recv_sem=recv_sems.at[sems],
            device_id=device,
            device_id_type=MESH,
        )

    def exchange(src, dst, own, sems):
        for offset in OFFSETS[: N - 1] if own else OFFSETS:
            t = device(offset)
            push(
                src.at[pl.ds(t, 1)],
                dst.at[pl.ds(me if own else N + me, 1)],
                (t, view if own else other),
                sems,
            ).start()

    def finish_send(src, own, sems):
        push(src, src, (me, view), sems).wait_send()

    def finish_recv(dst, own, sems):
        rows = pl.ds(0, N) if own else pl.ds(N, N)
        push(dst.at[rows], dst.at[rows], (me, view), sems).wait_recv()

    def keep(src, dst, spare, sems):
        mine = src.at[pl.ds(me, 1)]
        pltpu.make_async_copy(mine, dst.at[pl.ds(me, 1)], recv_sems.at[sems]).start()
        pltpu.make_async_copy(mine, spare, send_sems.at[sems]).start()

    exchange(ask, req, True, 0)
    keep(ask, req, spare_ask, 0)
    for load in [*small[1:], *loads]:
        load.wait()
    camera = [[cam_ref[r, 0, c] for c in range(4)] for r in range(2)]
    eye = [eye_ref[0, c] for c in range(3)]
    values = [pv[pl.ds(p, COLS, stride=PITCH), :] for p in range(ROWS)]
    for f, row in enumerate(project(values, camera, eye)):
        pj[f] = row

    sheet = jnp.zeros((8, 128), F32)
    spots = [(r, c, camera[r][c]) for r in range(2) for c in range(4)]
    spots += [(3, c, eye[c]) for c in range(3)]
    for r, c, number in spots:
        here = (iota((8, 128), 0) == r) & (iota((8, 128), 1) == c)
        sheet = jnp.where(here, number, sheet)
    cams_ref[0:8, :] = sheet
    greeting = pltpu.make_async_remote_copy(
        src_ref=cams_ref.at[pl.ds(0, 8)],
        dst_ref=cams_ref.at[pl.ds(8, 8)],
        send_sem=cam_sem.at[0],
        recv_sem=cam_sem.at[1],
        device_id=(me, other),
        device_id_type=MESH,
    )
    greeting.start()

    pixel = iota((TILES, PX), 1)
    u = (pixel % 16).astype(F32) - 7.5
    w = (pixel // 16).astype(F32) - 7.5
    basis = [jnp.ones_like(u), u, w, u * u, u * w, w * w]
    blank()
    for c in range(6):
        for part in range(3):
            lay(3 * c + part, GROUP, basis[c])
    rhs[...] = staged().astype(BF16)
    blank()
    for c in range(6):
        lay(c, MOMS, basis[c])
    both_rows[:, 0:PX] = staged(slice(0, 128)).astype(BF16)
    both_rows[:, PX : 2 * PX] = staged(slice(0, 128)).astype(BF16)
    for pair in places[1:]:
        for part in pair:
            part[...] = jnp.zeros(part.shape, F32)
    gsend[...] = jnp.zeros(gsend.shape, F32)

    for t in range(TILES):
        listed = lists_ref[t : t + 1, :]
        at_pos = iota((CAP, K), 0) == jnp.broadcast_to(listed & 15, (CAP, K))
        at_own = iota((N, K), 0) == jnp.broadcast_to(listed >> 4, (N, K))
        pos_ones[t] = jnp.where(at_pos, 1.0, 0.0).astype(BF16)
        own_ones[t] = jnp.where(at_own, 1.0, 0.0).astype(BF16)

    finish_recv(req, True, 0)
    wanted = req[0:N, :].T[0:CAP, :]
    wanted = jnp.concatenate([wanted[0:8], wanted[8:16]], axis=1)
    want_row, want_lane = wanted >> 7, wanted & 127
    for f in range(FEATS):
        found = pick(pj[f], want_row, want_lane)
        stage[CAP * f : CAP * f + 8, :] = found
        stage[CAP * f + 8 : CAP * (f + 1), :] = pltpu.roll(found, N, 1)
    rowsend[...] = stage[...].T[0:N, :]
    exchange(rowsend, rowsin, True, 2)
    keep(rowsend, rowsin, spare_rows, 2)

    passed = pltpu.make_async_remote_copy(
        src_ref=req.at[pl.ds(0, N)],
        dst_ref=req.at[pl.ds(N, N)],
        send_sem=send_sems.at[1],
        recv_sem=recv_sems.at[1],
        device_id=(me, other),
        device_id_type=MESH,
    )
    passed.start()

    entry_row = lists_ref[...] & 7
    entry_lane = (lists_ref[...] >> 4) + ((lists_ref[...] & 8) << 3)
    passed.wait_recv()
    finish_recv(rowsin, True, 2)
    stage[...] = rowsin[...].T

    entries = []
    for f in range(FEATS):
        first_half = stage[CAP * f : CAP * f + 8, :]
        second_half = stage[CAP * f + 8 : CAP * (f + 1), :]
        table = jnp.where(iota((8, 128), 1) < N, first_half, pltpu.roll(second_half, N, 1))
        entries.append(
            jnp.concatenate(
                [
                    pick(table, entry_row[:, h : h + 128], entry_lane[:, h : h + 128])
                    for h in (0, 128)
                ],
                axis=1,
            )
        )

    tile_row = iota((TILES, PX), 0)
    mid_x = jnp.zeros((TILES, PX), F32)
    mid_y = jnp.zeros((TILES, PX), F32)
    live = jnp.zeros((TILES, PX), jnp.int32)
    for t in range(TILES):
        here = tile_row == t
        mid_x = jnp.where(here, (tile_ref[0, t] % 32 * 16 + 8).astype(F32), mid_x)
        mid_y = jnp.where(here, (tile_ref[0, t] // 32 * 16 + 8).astype(F32), mid_y)
        live = jnp.where(here, count_ref[0, t], live)
    alive = pixel < live
    spot_x = entries[0] * 512.0 - mid_x
    spot_y = entries[1] * 512.0 - mid_y
    con_a, con_b, con_c = [entries[2 + i] * (1.0 / 262144.0) for i in range(3)]
    lin_x = con_a * spot_x + con_b * spot_y
    lin_y = con_c * spot_y + con_b * spot_x
    level = entries[5] - 0.5 * (spot_x * lin_x + spot_y * lin_y)
    coeffs = [level, lin_x, lin_y, -0.5 * con_a, -con_b, -0.5 * con_c]
    for c in range(6):
        coeff = jnp.where(alive, coeffs[c] * LOG2E, -1e30 if c == 0 else 0.0)
        for part, piece in enumerate(split(coeff, 3)):
            lay(3 * c + part, GROUP, piece, 1)
    colours = [jnp.where(alive, entries[6 + c], 0.0) for c in range(3)]
    for c in range(3):
        high, low, rest = split(colours[c], 3)
        for part, piece in enumerate((high, high, low)):
            lay(18 + 3 * c + part, GROUP, piece, 1)
        lay(27 + c, GROUP, rest, 1)
    lanes[...] = staged(where=1).T

    column = iota((TILES * GROUP, 3 * 128), 0) % GROUP
    wants = iota((TILES * GROUP, 3 * 128), 1) // 128
    adds = (column == 18 + 3 * wants) | (column == 20 + 3 * wants) | (column == 27 + wants)
    chooser = jnp.where(adds, 1.0, 0.0).astype(BF16)
    group_mask = iota((TILES, TILES * GROUP), 1) // GROUP == iota((TILES, TILES * GROUP), 0)

    def chunk_rows(chunk):
        return slice(chunk * CHUNK * TILES, (chunk + 1) * CHUNK * TILES)

    def operands(chunk):
        line = lanes[chunk * CHUNK : (chunk + 1) * CHUNK, :]
        spread = jnp.where(group_mask[None], line[:, None, :], 0.0)
        lhs[chunk_rows(chunk), :] = spread.reshape(CHUNK * TILES, TILES * GROUP).astype(BF16)

    def exponents(chunk):
        rows = chunk_rows(chunk)
        power = jnp.dot(lhs[rows, :], rhs[...], preferred_element_type=F32)
        alphas[rows, :] = jnp.exp2(power)
        paints[rows, :] = jnp.dot(lhs[rows, :], chooser, preferred_element_type=F32)

    through = jnp.ones((TILES, PX), F32)
    images = [jnp.zeros((TILES, PX), F32)] * 3
    chunks = K // CHUNK
    for stage_no in range(chunks + 2):
        if stage_no < chunks:
            operands(stage_no)
        if 1 <= stage_no <= chunks:
            exponents(stage_no - 1)
        if stage_no >= 2:
            first = (stage_no - 2) * CHUNK * TILES
            for i in range(0, CHUNK, 2):
                pair = []
                for j in (i, i + 1):
                    at = slice(first + j * TILES, first + (j + 1) * TILES)
                    alpha = alphas[at, :]
                    weight = through * alpha
                    through = through * (1.0 - alpha)
                    weights[at, :] = weight
                    pair.append(weight)
                    for c in range(3):
                        paint = paints[at, 128 * c : 128 * c + 128]
                        images[c] = images[c] + weight * jnp.concatenate([paint, paint], axis=1)
                at = slice(first + i * TILES, first + (i + 2) * TILES)
                high, low = split_low(jnp.concatenate(pair, axis=0), 2)
                pieces[at, 2 * PX : 3 * PX] = high
                pieces[at, 3 * PX : 4 * PX] = low

    for c in range(3):
        rendered_ref[c] = images[c]
        shade = (images[c] - target_ref[c]) * (1.0 / 256.0)
        high, low = split(shade, 2)
        for part, piece in enumerate((high, low, high)):
            lay(18 + 3 * c + part, GROUP, piece, 2)
        for part, piece in enumerate(split(shade, 3)):
            lay(6 + 3 * c + part, MOMS, piece, 3)
    rhs[...] = staged(where=2).astype(BF16)
    both_rows[:, 2 * PX : 3 * PX] = staged(where=3).astype(BF16)
    both_rows[:, 3 * PX : 4 * PX] = staged(where=3).astype(BF16)

    def tone_of(chunk):
        rows = chunk_rows(chunk)
        tones[rows, :] = jnp.dot(lhs[rows, :], rhs[...], preferred_element_type=F32)

    def reductions(chunk):
        rows = chunk_rows(chunk)
        totals[rows, :] = dot_nt(pieces[rows, :], both_rows[...])

    behind = jnp.zeros((TILES, PX), F32)
    for stage_no in range(chunks + 2):
        if stage_no < chunks:
            tone_of(chunks - 1 - stage_no)
        if stage_no >= 2:
            reductions(chunks + 1 - stage_no)
        if 1 <= stage_no <= chunks:
            first = (chunks - stage_no) * CHUNK * TILES
            for i in reversed(range(0, CHUNK, 2)):
                pair = [None, None]
                for j in (1, 0):
                    at = slice(first + (i + j) * TILES, first + (i + j + 1) * TILES)
                    tone, alpha = tones[at, :], alphas[at, :]
                    pair[j] = weights[at, :] * (tone - behind)
                    behind = behind * (1.0 - alpha) + alpha * tone
                at = slice(first + i * TILES, first + (i + 2) * TILES)
                high, low = split_low(jnp.concatenate(pair, axis=0), 2)
                pieces[at, 0:PX] = high
                pieces[at, PX : 2 * PX] = low

    group = iota((K, 128), 1) // MOMS
    sums = totals[pl.ds(0, K, stride=TILES), :]
    for t in range(1, TILES):
        sums = jnp.where(group == t, totals[pl.ds(t, K, stride=TILES), :], sums)
    turned_sums = sums.T
    stage[0:128, :] = turned_sums[:, 0:128]
    stage_hi[0:128, :] = turned_sums[:, 128:256]
    sums = [take(c, MOMS) for c in range(15)]
    s_1, s_u, s_w, s_uu, s_uw, s_ww = sums[0:6]
    d_x = s_u - spot_x * s_1
    d_y = s_w - spot_y * s_1
    d_xx = s_uu - 2.0 * spot_x * s_u + spot_x * spot_x * s_1
    d_yy = s_ww - 2.0 * spot_y * s_w + spot_y * spot_y * s_1
    d_xy = s_uw - spot_x * s_w - spot_y * s_u + spot_x * spot_y * s_1
    slopes = [
        512.0 * (con_a * d_x + con_b * d_y),
        512.0 * (con_c * d_y + con_b * d_x),
        d_xx * (-0.5 / 262144.0),
        d_xy * (-1.0 / 262144.0),
        d_yy * (-0.5 / 262144.0),
        s_1,
        *[sums[6 + 3 * c] + sums[7 + 3 * c] + sums[8 + 3 * c] for c in range(3)],
    ]
    for f in range(FEATS):
        for part, piece in enumerate(split(jnp.where(alive, slopes[f], 0.0), 2)):
            lay(FEATS * part + f, GROUP, piece)

    total = jnp.zeros((2 * FEATS * CAP, N), F32)
    for t in range(TILES):
        block = staged(slice(t * GROUP, t * GROUP + 2 * FEATS)).astype(BF16)
        left = block[:, None, :] * pos_ones[t][None]
        total = total + dot_nt(left.reshape(2 * FEATS * CAP, K), own_ones[t])
    size = FEATS * CAP
    summed = total[0:size] + total[size : 2 * size]
    gsend[:, 0:size] = summed.T

    for offset in OFFSETS:
        t = device(offset)
        for own_view in (True, False):
            if any(offset) or not own_view:
                push(
                    gsend.at[pl.ds(t, 1)],
                    gin.at[pl.ds(me if own_view else N + me, 1)],
                    (t, view if own_view else other),
                    3 if own_view else 4,
                ).start()
    keep(gsend, gin, spare_grads, 3)

    turned[...] = req[...].T[0:CAP, :]

    def locate(j, found):
        line = turned[pl.ds(j, 1), :]
        line_hi, line_lo = line >> 7, line & 127
        hit = iota((COLS, 128), 0) == jnp.broadcast_to(line_hi, (COLS, 128))
        spot = iota((COLS, 128), 1).astype(F32)
        digits = jnp.concatenate(
            [
                jnp.where(hit, j.astype(F32), 0.0),
                jnp.where(hit, spot, 0.0),
            ],
            axis=0,
        ).astype(BF16)
        ones = jnp.where(
            iota((128, 128), 0) == jnp.broadcast_to(line_lo, (128, 128)), 1.0, 0.0
        ).astype(BF16)
        return found + dot_nt(digits, ones)

    found = lax.fori_loop(0, CAP, locate, jnp.zeros((2 * COLS, 128), F32), unroll=4)
    found_row = found[0:COLS].astype(jnp.int32)
    found_lane = found[COLS : 2 * COLS].astype(jnp.int32)
    own = found_lane < N

    greeting.wait_recv()

    def chosen(row, col):
        return jnp.where(
            own,
            jnp.broadcast_to(cams_ref[row : row + 1, col : col + 1], own.shape),
            jnp.broadcast_to(cams_ref[8 + row : 9 + row, col : col + 1], own.shape),
        )

    camera = [[chosen(r, c) for c in range(4)] for r in range(2)]
    eye = [chosen(3, c) for c in range(3)]
    values = [pv[pl.ds(p, COLS, stride=PITCH), :] for p in range(ROWS)]
    _, pull = jax.vjp(lambda rows: project(rows, camera, eye), values)

    finish_recv(gin, True, 3)
    finish_recv(gin, False, 4)
    stage[...] = gin[...].T

    found = [
        pick(stage[CAP * f : CAP * (f + 1), :], found_row, found_lane) for f in range(FEATS)
    ]
    (grads,) = pull(found)
    for p in range(ROWS):
        grads_ref[pl.ds(p, COLS, stride=PITCH), :] = grads[p]
    finish_send(ask, True, 0)
    passed.wait_send()
    finish_send(rowsend, True, 2)
    finish_send(gsend, True, 3)
    finish_send(gsend, False, 4)
    greeting.wait_send()


def hand_on(image_ref, blocks_ref, image_hbm, grads_hbm, sems):
    copies = [
        pltpu.make_async_copy(
            blocks_ref.at[pl.ds(PITCH * b, ROWS)], grads_hbm.at[:, pl.ds(128 * b, 128)], sems.at[b]
        )
        for b in range(COLS)
    ]
    copies.append(pltpu.make_async_copy(image_ref, image_hbm, sems.at[COLS]))
    for copy in copies:
        copy.start()
    for copy in copies:
        copy.wait()


def on_device(params, camera, eye_point, tile_of, fetch, lists, counts, target):
    vmem = pl.BlockSpec(memory_space=pltpu.VMEM)
    hbm = pl.BlockSpec(memory_space=pltpu.HBM)
    image, blocks = pl.pallas_call(
        render_kernel,
        out_shape=(
            pltpu.VMEM((3, TILES, PX), F32),
            pltpu.VMEM((COLS * PITCH, 128), F32),
        ),
        in_specs=[hbm] * 8,
        out_specs=(vmem, vmem),
        scratch_shapes=[
            pltpu.VMEM((16, 128), F32),
            pltpu.SMEM((3, 1, 4), F32),
            pltpu.SMEM((1, 3), F32),
            pltpu.SMEM((1, TILES), jnp.int32),
            pltpu.SMEM((1, TILES), jnp.int32),
            pltpu.VMEM((CAP, N), jnp.int32),
            pltpu.VMEM((TILES, K), jnp.int32),
            pltpu.VMEM((3, TILES, PX), F32),
            pltpu.VMEM((COLS * PITCH, 128), F32),
            pltpu.VMEM((FEATS, COLS, 128), F32),
            pltpu.VMEM((N, 128), jnp.int32),
            pltpu.VMEM((2 * N, 128), jnp.int32),
            pltpu.VMEM((N, 256), F32),
            pltpu.VMEM((2 * N, 256), F32),
            pltpu.VMEM((256, 128), F32),
            pltpu.VMEM((256, 128), F32),
            pltpu.VMEM((K * TILES, 256), BF16),
            pltpu.VMEM((256, PX), BF16),
            pltpu.VMEM((K * TILES, PX), F32),
            pltpu.VMEM((K * TILES, PX), F32),
            pltpu.VMEM((K, 256), F32),
            pltpu.VMEM((N, 256), F32),
            pltpu.VMEM((2 * N, 256), F32),
            pltpu.VMEM((CAP, 128), jnp.int32),
            pltpu.VMEM((1, 128), jnp.int32),
            pltpu.VMEM((1, 256), F32),
            pltpu.VMEM((1, 256), F32),
            pltpu.VMEM((TILES, CAP, K), BF16),
            pltpu.VMEM((TILES, N, K), BF16),
            pltpu.VMEM((K * TILES, 128), F32),
            pltpu.VMEM((TILES * GROUP, 128), F32),
            pltpu.VMEM((TILES * GROUP, 128), F32),
            pltpu.VMEM((TILES * GROUP, 128), F32),
            pltpu.VMEM((TILES * GROUP, 128), F32),
            pltpu.VMEM((TILES * MOMS, 128), F32),
            pltpu.VMEM((TILES * MOMS, 128), F32),
            pltpu.VMEM((TILES * MOMS, 4 * PX), BF16),
            pltpu.VMEM((K * TILES, PX), F32),
            pltpu.VMEM((K * TILES, 3 * 128), F32),
            pltpu.VMEM((K * TILES, 4 * PX), BF16),
            pltpu.SemaphoreType.DMA((7,)),
            pltpu.SemaphoreType.DMA((2,)),
            pltpu.SemaphoreType.DMA((COLS,)),
            pltpu.SemaphoreType.DMA((5,)),
            pltpu.SemaphoreType.DMA((5,)),
        ],
        compiler_params=pltpu.CompilerParams(
            collective_id=0, has_side_effects=True, vmem_limit_bytes=40 << 20
        ),
        name="render",
    )(
        *[
            pltpu.with_memory_space_constraint(arg, pltpu.HBM)
            for arg in (
                params,
                camera.transpose(1, 0, 2),
                eye_point,
                tile_of,
                counts,
                fetch[0, 0].T,
                lists[0],
                target[0].transpose(1, 0, 2),
            )
        ]
    )
    rendered, grads = pl.pallas_call(
        hand_on,
        out_shape=(
            jax.ShapeDtypeStruct(image.shape, F32),
            jax.ShapeDtypeStruct(params.shape, F32),
        ),
        in_specs=[pl.BlockSpec(memory_space=pl.ANY)] * 2,
        out_specs=(hbm, hbm),
        scratch_shapes=[pltpu.SemaphoreType.DMA((COLS + 1,))],
        compiler_params=pltpu.CompilerParams(vmem_limit_bytes=4 << 20),
        name="hand_on",
    )(*[pltpu.with_memory_space_constraint(x, pltpu.VMEM) for x in (image, blocks)])
    return (rendered.transpose(1, 0, 2)[None], grads)


def solution(mesh):
    placed = (
        P(None, "space"),
        P("view", None, None),
        P("view", None),
        P("view", "space"),
        P("view", "space", None, None),
        P("view", "space", None),
        P("view", "space"),
        P("view", "space", None, None),
    )
    return jax.shard_map(
        on_device,
        mesh=mesh,
        in_specs=placed,
        out_specs=(P("view", "space", None, None), P(None, "space")),
        check_vma=False,
    )
```
